32 devices in a mesh: seq: 8 (over z, x), tp: 4 (over y, core).
Axes of the slice: x: 2, y: 2, z: 4, core: 2. Of those that a mesh axis runs over, the one named last changes fastest.
Arguments:
- inputs: bfloat16 [6144, 2048], P(('seq', 'tp')), may hold values from -6 to 6
- out_grad: bfloat16 [6144, 2048], P(('seq', 'tp')), may hold values from -6 to 6
- seq_lengths: int32 [2], replicated, may hold values from 1025 to 4864, as said below
- log_decay: float32 [6144, 16], P('seq', 'tp'), may hold values from -1 to 0, as said below
- mixer_weight: float32 [4, 2048, 2048], P(None, 'seq', 'tp'), may hold values from -0.125 to 0.125
- output_weight: float32 [2048, 2048], P('tp', 'seq'), may hold values from -0.125 to 0.125
- glu_weight: float32 [2, 2048, 5632], P(None, 'seq', 'tp'), may hold values from -0.125 to 0.125
- down_weight: float32 [5632, 2048], P('tp', 'seq'), may hold values from -0.078125 to 0.078125
- mixer_first: float32 [4, 2048, 2048], P(None, 'seq', 'tp'), may hold values from -40 to 40
- output_first: float32 [2048, 2048], P('tp', 'seq'), may hold values from -40 to 40
- glu_first: float32 [2, 2048, 5632], P(None, 'seq', 'tp'), may hold values from -40 to 40
- down_first: float32 [5632, 2048], P('tp', 'seq'), may hold values from -40 to 40
- mixer_second: float32 [4, 2048, 2048], P(None, 'seq', 'tp'), may hold values from 92.16 to 1228.8
- output_second: float32 [2048, 2048], P('tp', 'seq'), may hold values from 92.16 to 1228.8
- glu_second: float32 [2, 2048, 5632], P(None, 'seq', 'tp'), may hold values from 92.16 to 1228.8
- down_second: float32 [5632, 2048], P('tp', 'seq'), may hold values from 92.16 to 1228.8
Outputs:
- block_out: bfloat16 [6144, 2048], P(('seq', 'tp'))
- input_grad: float32 [6144, 2048], P(('seq', 'tp'))
- mixer_new: float32 [4, 2048, 2048], P(None, 'seq', 'tp')
- output_new: float32 [2048, 2048], P('tp', 'seq')
- glu_new: float32 [2, 2048, 5632], P(None, 'seq', 'tp')
- down_new: float32 [5632, 2048], P('tp', 'seq')
- mixer_first_new: float32 [4, 2048, 2048], P(None, 'seq', 'tp')
- output_first_new: float32 [2048, 2048], P('tp', 'seq')
- glu_first_new: float32 [2, 2048, 5632], P(None, 'seq', 'tp')
- down_first_new: float32 [5632, 2048], P('tp', 'seq')
- mixer_second_new: float32 [4, 2048, 2048], P(None, 'seq', 'tp')
- output_second_new: float32 [2048, 2048], P('tp', 'seq')
- glu_second_new: float32 [2, 2048, 5632], P(None, 'seq', 'tp')
- down_second_new: float32 [5632, 2048], P('tp', 'seq')
The draws below stay inside these ranges and needn't reach their ends.
Inputs may be any that keep to these rules, and one draw needn't show every extreme that they name: `seq_lengths`: sequence i fills ceil(count / 256) consecutive blocks, sequences in order from block 0 and together filling all 24 blocks; each fills 5 to 19 blocks, and one is exactly 4864 rows long. `log_decay`: every entry is negative.
All inputs are finite; a program needn't handle non-finite values.
Results may differ from the reference program's by a relative error of at most 0.014.
Values may be sent and summed in bfloat16 or wider, within the bound.
No kernel may reach another device: no remote copies, remote signals or barrier semaphores. Data moves between devices by JAX's collectives and lax.ppermute only.
A program may use at most 320 MiB of HBM per device.

```python
import math
import jax
import jax.numpy as jnp
from jax import lax

D = 2048
HEAD_TOTAL = 16
HD = 128
FF = 5632
BLK = 256
MINB = 5
STEP = 10
NBLK = 24
TOKEN_ROWS_ALL = 6144
NSEQ = 2
MAXB = 19


def draw_seq_lengths(key, part):
    key_entries = jax.random.split(jax.random.fold_in(key, 7), 5)
    others = NSEQ - 1
    spare = NBLK - MAXB - MINB * others
    order = jax.random.permutation(key_entries[0], others)
    counts = MINB + spare // others + (order < spare % others).astype(jnp.int32)
    pairs = others // 2
    shuffled = jax.random.permutation(key_entries[1], others)
    donors = shuffled[0:2 * pairs:2]
    takers = shuffled[1:2 * pairs:2]
    headroom = jnp.minimum(counts[donors] - MINB, MAXB - counts[takers])
    shifted = jax.random.randint(key_entries[2], (pairs,), 0, headroom + 1)
    counts = counts.at[donors].add(-shifted).at[takers].add(shifted)
    longest = jax.random.randint(key_entries[3], (), 0, NSEQ)
    positions = jnp.arange(NSEQ, dtype=jnp.int32)
    source = jnp.clip(positions - (positions > longest).astype(jnp.int32), 0, others - 1)
    blocks = jnp.where(positions == longest, MAXB, counts[source])
    last_fill = jax.random.randint(key_entries[4], (NSEQ,), 1, BLK + 1)
    lengths = (blocks - 1) * BLK + last_fill
    return jnp.where(positions == longest, MAXB * BLK, lengths).astype(jnp.int32)


def draw_log_decay(key, part):
    key_entries = jax.random.split(jax.random.fold_in(key, 11), 6)
    fast_share = 0.5
    fast_heads = jax.random.uniform(key_entries[0], (HEAD_TOTAL,)) < fast_share
    fast_rates = jax.random.uniform(key_entries[1], (HEAD_TOTAL,), minval=1.0 / 50.0, maxval=1.0 / 30.0)
    slow_rates = jax.random.uniform(key_entries[2], (HEAD_TOTAL,), minval=0.25, maxval=1.0) / TOKEN_ROWS_ALL
    decay_rates = jnp.where(fast_heads, fast_rates, slow_rates)
    jaggedness = jnp.exp(jax.random.uniform(key_entries[3], (TOKEN_ROWS_ALL, HEAD_TOTAL), minval=-0.7, maxval=0.7))
    spike_values = jax.random.uniform(key_entries[4], (TOKEN_ROWS_ALL, HEAD_TOTAL)) < 3.0 / TOKEN_ROWS_ALL
    spike_loss_value = jnp.log(jax.random.uniform(key_entries[5], (TOKEN_ROWS_ALL, HEAD_TOTAL), minval=0.5, maxval=0.8))
    return (jnp.where(spike_values, spike_loss_value, 0.0) - decay_rates[None, :] * jaggedness).astype(jnp.float32)


def block_levels(key, dims, shards, smallest, top_value):
    def one(axis_at, blocks):
        heights = jax.random.uniform(jax.random.fold_in(jax.random.fold_in(key, 6), axis_at), (blocks,), jnp.float32, smallest / len(shards), top_value / len(shards))
        return jnp.repeat(jnp.exp(heights), dims[axis_at] // blocks).reshape((-1,) + (1,) * (len(dims) - axis_at - 1))

    gain = one(*shards[0])
    for cut in shards[1:]:
        gain = gain * one(*cut)
    return gain


def scatter_about(rng, dims, spread, limit, shards=(), kind=jnp.bfloat16):
    values = spread * jax.random.normal(rng, dims, jnp.float32)
    if shards:
        values = values * block_levels(rng, dims, shards, -0.22, 0.18)
    return jnp.clip(values, -limit, limit).astype(kind)


def setup_inputs(seed: int = 0) -> dict:
    key_of = jax.random.split(jax.random.key(seed), 17)
    inputs = scatter_about(key_of[0], (TOKEN_ROWS_ALL, D), 1.0, 6.0, ((0, 32),))
    out_grad = scatter_about(key_of[1], (TOKEN_ROWS_ALL, D), 1.0, 6.0, ((0, 32),))
    seq_lengths = draw_seq_lengths(jax.random.fold_in(key_of[16], 71), 0)
    log_decay = draw_log_decay(jax.random.fold_in(key_of[16], 71), 0)
    mixer_weight = scatter_about(key_of[4], (4, D, D), D ** -0.5, 0.125, ((1, 8), (2, 4)), jnp.float32)
    output_weight = scatter_about(key_of[5], (D, D), D ** -0.5, 0.125, ((0, 4), (1, 8)), jnp.float32)
    glu_weight = scatter_about(key_of[6], (2, D, FF), D ** -0.5, 0.125, ((1, 8), (2, 4)), jnp.float32)
    down_weight = scatter_about(key_of[7], (FF, D), FF ** -0.5, 0.078125, ((0, 4), (1, 8)), jnp.float32)
    mixer_first = scatter_about(key_of[8], (4, D, D), (0.08 * TOKEN_ROWS_ALL ** 0.5), 40.0, ((1, 8), (2, 4)), jnp.float32)
    output_first = scatter_about(key_of[9], (D, D), (0.08 * TOKEN_ROWS_ALL ** 0.5), 40.0, ((0, 4), (1, 8)), jnp.float32)
    glu_first = scatter_about(key_of[10], (2, D, FF), (0.08 * TOKEN_ROWS_ALL ** 0.5), 40.0, ((1, 8), (2, 4)), jnp.float32)
    down_first = scatter_about(key_of[11], (FF, D), (0.08 * TOKEN_ROWS_ALL ** 0.5), 40.0, ((0, 4), (1, 8)), jnp.float32)
    mixer_second = jnp.clip(jnp.exp(math.log(1228.8) - 2.5902672 * jax.random.uniform(key_of[12], (4, D, D), jnp.float32) ** block_levels(key_of[12], (4, D, D), ((1, 8), (2, 4)), -0.2, 0.2)), 92.16, 1228.8)
    output_second = jnp.clip(jnp.exp(math.log(1228.8) - 2.5902672 * jax.random.uniform(key_of[13], (D, D), jnp.float32) ** block_levels(key_of[13], (D, D), ((0, 4), (1, 8)), -0.2, 0.2)), 92.16, 1228.8)
    glu_second = jnp.clip(jnp.exp(math.log(1228.8) - 2.5902672 * jax.random.uniform(key_of[14], (2, D, FF), jnp.float32) ** block_levels(key_of[14], (2, D, FF), ((1, 8), (2, 4)), -0.2, 0.2)), 92.16, 1228.8)
    down_second = jnp.clip(jnp.exp(math.log(1228.8) - 2.5902672 * jax.random.uniform(key_of[15], (FF, D), jnp.float32) ** block_levels(key_of[15], (FF, D), ((0, 4), (1, 8)), -0.2, 0.2)), 92.16, 1228.8)
    return {"inputs": inputs, "out_grad": out_grad, "seq_lengths": seq_lengths, "log_decay": log_decay, "mixer_weight": mixer_weight, "output_weight": output_weight, "glu_weight": glu_weight, "down_weight": down_weight, "mixer_first": mixer_first, "output_first": output_first, "glu_first": glu_first, "down_first": down_first, "mixer_second": mixer_second, "output_second": output_second, "glu_second": glu_second, "down_second": down_second}


NORM_EPS = 1e-06
BETA_ONE = 0.9
BETA_TWO = 0.95
ADAM_EPS = 1e-08
WEIGHT_DECAY = 0.1
LEARN_RATE = 0.02
HIGH = lax.Precision.HIGHEST

@jax.custom_vjp
def low(v):
    return lax.optimization_barrier(v.astype(jnp.bfloat16)).astype(jnp.float32)

@jax.custom_vjp
def low_back(v):
    return v

def low_keep(v):
    return (low(v), None)

def low_pass(kept, grad):
    return (grad,)

def back_keep(v):
    return (v, None)

def back_low(kept, grad):
    return (low(grad),)
low.defvjp(low_keep, low_pass)
low_back.defvjp(back_keep, back_low)

def layout(seq_lengths, first_block, block_count):
    blocks = ((seq_lengths + BLK - 1) // BLK).astype(jnp.int32)
    starts = (jnp.cumsum(blocks) - blocks).astype(jnp.int32)
    block_index = (first_block + jnp.arange(block_count, dtype=jnp.int32)).astype(jnp.int32)
    begins = starts[None, :] == block_index[:, None]
    keep_flags = 1.0 - jnp.any(begins, axis=1).astype(jnp.float32)
    owner_index = (lax.optimization_barrier(jnp.sum((starts[None, :] <= block_index[:, None]).astype(jnp.int32), axis=1)) - 1).astype(jnp.int32)
    chosen = jnp.arange(seq_lengths.shape[0], dtype=jnp.int32)[None, :] == owner_index[:, None]
    own_start = lax.optimization_barrier(jnp.sum(jnp.where(chosen, starts[None, :], 0), axis=1)).astype(jnp.int32)
    own_length = lax.optimization_barrier(jnp.sum(jnp.where(chosen, seq_lengths[None, :], 0), axis=1)).astype(jnp.int32)
    position = (block_index - own_start)[:, None] * BLK + jnp.arange(BLK, dtype=jnp.int32)[None, :]
    token_mask = position < own_length[:, None]
    return (keep_flags, token_mask.reshape(block_count * BLK))

def normalize(values):
    return values * lax.rsqrt(lax.optimization_barrier(jnp.mean(values * values, axis=-1, keepdims=True)) + NORM_EPS)

def mixer_block(carried, inputs):
    query_rows, key_rows, value_rows, cumulative, keep_flag = inputs
    block_ends = cumulative[-1]
    causal = jnp.arange(BLK)[:, None] >= jnp.arange(BLK)[None, :]
    log_gaps = jnp.minimum(cumulative[:, None, :] - cumulative[None, :, :], 0.0)
    decays = jnp.where(causal[:, :, None], jnp.exp(log_gaps), 0.0)
    scores = low_back(jnp.einsum('the,she->tsh', query_rows, key_rows, precision=HIGH))
    block_probs = low(scores * decays)
    inner_part = jnp.einsum('tsh,shf->thf', block_probs, value_rows, precision=HIGH)
    used_state = keep_flag * carried
    scaled_q = low(query_rows * jnp.exp(cumulative)[:, :, None])
    outer_part = jnp.einsum('the,hef->thf', scaled_q, low(used_state), precision=HIGH)
    scaled_k = low(key_rows * jnp.exp(block_ends[None, :] - cumulative)[:, :, None])
    state_terms = low_back(jnp.einsum('she,shf->hef', scaled_k, value_rows, precision=HIGH))
    renewed = jnp.exp(block_ends)[:, None, None] * used_state + state_terms
    return (renewed, inner_part + outer_part)

def forward(inputs_f, mixer_weight, output_weight, glu_weight, down_weight, cumulative, keep_flags, token_mask):
    rows_one = low(normalize(inputs_f))
    projected = jnp.einsum('td,jdc->jtc', rows_one, low(mixer_weight), precision=HIGH)
    queries = low(jax.nn.silu(low_back(projected[0])))
    keys_all = low(jax.nn.silu(low_back(projected[1]))) * token_mask[:, None]
    values_all = low(low_back(projected[2])) * token_mask[:, None]
    gate_u = low_back(projected[3])
    block_shape = (NBLK, BLK, HEAD_TOTAL, HD)
    zero_state = jnp.zeros((HEAD_TOTAL, HD, HD), jnp.float32)
    last_state, mixer_out = lax.scan(jax.checkpoint(mixer_block), zero_state, (queries.reshape(block_shape), keys_all.reshape(block_shape), values_all.reshape(block_shape), cumulative, keep_flags))
    mixer_out = low_back(mixer_out.reshape(TOKEN_ROWS_ALL, D))
    joined = low(normalize(mixer_out) * gate_u)
    branch = low_back(jnp.dot(joined, low(output_weight), precision=HIGH))
    middle = inputs_f + branch
    rows_two = low(normalize(middle))
    glu_gates = jnp.einsum('td,jdc->jtc', rows_two, low(glu_weight), precision=HIGH)
    product = low(low_back(glu_gates[0]) * low_back(glu_gates[1]))
    feed_out = low_back(jnp.dot(product, low(down_weight), precision=HIGH))
    return middle + feed_out

def adamw_step(weight, first, second, gradient):
    first_new = BETA_ONE * first + (1.0 - BETA_ONE) * gradient
    second_new = BETA_TWO * second + (1.0 - BETA_TWO) * gradient * gradient
    fix_one = 1.0 - BETA_ONE ** STEP
    fix_two = 1.0 - BETA_TWO ** STEP
    update = first_new / fix_one / (jnp.sqrt(second_new / fix_two) + ADAM_EPS)
    return (weight - LEARN_RATE * (update + WEIGHT_DECAY * weight), first_new, second_new)

def reference(inputs, out_grad, seq_lengths, log_decay, mixer_weight, output_weight, glu_weight, down_weight, mixer_first, output_first, glu_first, down_first, mixer_second, output_second, glu_second, down_second):
    keep_flags, token_mask = layout(seq_lengths, 0, NBLK)
    token_mask = token_mask.astype(jnp.float32)
    cumulative = jnp.cumsum(log_decay.reshape(NBLK, BLK, HEAD_TOTAL), axis=1)
    inputs_f = inputs.astype(jnp.float32)

    def layer_fn(inp, mix_w, out_w, glu_w, down_w):
        return forward(inp, mix_w, out_w, glu_w, down_w, cumulative, keep_flags, token_mask)
    result, pullback = jax.vjp(layer_fn, inputs_f, mixer_weight, output_weight, glu_weight, down_weight)
    input_grad, mixer_grad, output_grad, glu_grad, down_grad = pullback(out_grad.astype(jnp.float32))
    mixer_new, mixer_first_new, mixer_second_new = adamw_step(mixer_weight, mixer_first, mixer_second, mixer_grad)
    output_new, output_first_new, output_second_new = adamw_step(output_weight, output_first, output_second, output_grad)
    glu_new, glu_first_new, glu_second_new = adamw_step(glu_weight, glu_first, glu_second, glu_grad)
    down_new, down_first_new, down_second_new = adamw_step(down_weight, down_first, down_second, down_grad)
    return (result.astype(jnp.bfloat16), input_grad, mixer_new, output_new, glu_new, down_new, mixer_first_new, output_first_new, glu_first_new, down_first_new, mixer_second_new, output_second_new, glu_second_new, down_second_new)
```

```python
import jax
import jax.numpy as jnp
from jax import lax
from jax.sharding import PartitionSpec as P

D = 2048
HD = 128
BLK = 256
STEP = 10


NORM_EPS = 1e-06
BETA_ONE = 0.9
BETA_TWO = 0.95
ADAM_EPS = 1e-08
WEIGHT_DECAY = 0.1
LEARN_RATE = 0.02

bf16 = jnp.bfloat16
f32 = jnp.float32


class Ring:
    def __init__(self, size):
        self.size = size
        self.order = [*range(0, size, 2), *range(size - 1, 0, -2)]
        after = {a: self.order[(i + 1) % size] for i, a in enumerate(self.order)}
        self.perms = ([(a, b) for a, b in after.items()], [(b, a) for a, b in after.items()])
        self.arrived = ([], [])

    def place(self):
        spot = [0] * self.size
        for i, a in enumerate(self.order):
            spot[a] = i
        here = jnp.asarray(spot, jnp.int32)[lax.axis_index("seq")]
        table = jnp.asarray(self.order, jnp.int32)
        half = self.size // 2
        self.owner = {
            off: table[lax.rem(here + off + self.size, self.size)]
            for off in range(1 - half, half + 1)
        }

    def send(self, value, way):
        past = self.arrived[way]
        if len(past) >= 2:
            value, _ = lax.optimization_barrier((value, past[-2]))
        value = lax.ppermute(value, "seq", self.perms[way])
        past.append(value)
        return value


def spread(ring, shard, axis, cut):
    size, half = ring.size, ring.size // 2
    wide = shard.shape[axis]
    shape = list(shard.shape)
    shape[axis] = wide * size
    whole = jnp.zeros(shape, shard.dtype)

    def put(whole, piece, off, shift=None):
        at = [0] * shard.ndim
        at[axis] = ring.owner[off] * wide
        if shift is not None:
            at[cut] = at[cut] + shift
        return lax.dynamic_update_slice(whole, piece, at)

    whole = put(whole, shard, 0)
    up = down = shard
    for k in range(1, half):
        up, down = ring.send(up, 0), ring.send(down, 1)
        whole = put(whole, up, -k)
        whole = put(whole, down, k)
        yield
    mid = shard.shape[cut] // 2
    first = lax.slice_in_dim(up, 0, mid, axis=cut)
    second = lax.slice_in_dim(down, mid, shard.shape[cut], axis=cut)
    first, second = ring.send(first, 0), ring.send(second, 1)
    whole = put(whole, first, half, 0)
    whole = put(whole, second, half, mid)
    return whole


def collect(ring, own, cut):
    half = ring.size // 2
    far = own(half).astype(bf16)
    mid = far.shape[cut] // 2
    up = ring.send(lax.slice_in_dim(far, 0, mid, axis=cut), 0)
    down = ring.send(lax.slice_in_dim(far, mid, far.shape[cut], axis=cut), 1)
    yield
    for k in range(half - 1, 0, -1):
        above, below = own(k), own(-k)
        pads = [(0, 0)] * above.ndim
        if k == half - 1:
            pads[cut] = (0, above.shape[cut] - mid)
            up = jnp.pad(up, pads)
            pads[cut] = (mid, 0)
            down = jnp.pad(down, pads)
        up = ring.send((above + up.astype(f32)).astype(bf16), 0)
        down = ring.send((below + down.astype(f32)).astype(bf16), 1)
        if k > 1:
            yield
    return own(0) + up.astype(f32) + down.astype(f32)


def in_turn(*work):
    done = [None] * len(work)
    left = list(range(len(work)))
    while left:
        for i in list(left):
            try:
                next(work[i])
            except StopIteration as end:
                done[i] = end.value
                left.remove(i)
    return done


def layout(seq_lengths, first_block, block_count):
    blocks = (seq_lengths + BLK - 1) // BLK
    count = seq_lengths.shape[0]
    earlier = jnp.arange(count)[:, None] > jnp.arange(count)[None, :]
    starts = jnp.sum(jnp.where(earlier, blocks[None, :], 0), axis=1)
    block_index = first_block + jnp.arange(block_count, dtype=jnp.int32)
    begins = starts[None, :] == block_index[:, None]
    keep_flags = 1.0 - jnp.any(begins, axis=1).astype(jnp.float32)
    owner_index = jnp.sum((starts[None, :] <= block_index[:, None]).astype(jnp.int32), axis=1) - 1
    chosen = jnp.arange(count, dtype=jnp.int32)[None, :] == owner_index[:, None]
    own_start = jnp.sum(jnp.where(chosen, starts[None, :], 0), axis=1)
    own_length = jnp.sum(jnp.where(chosen, seq_lengths[None, :], 0), axis=1)
    position = (block_index - own_start)[:, None] * BLK + jnp.arange(BLK, dtype=jnp.int32)[None, :]
    token_mask = position < own_length[:, None]
    return (keep_flags, token_mask.reshape(block_count * BLK))


def normalize(values):
    norm_scale = lax.rsqrt(jnp.mean(values * values, axis=-1, keepdims=True) + NORM_EPS)
    return (values * norm_scale, norm_scale)


def norm_back(normed, norm_scale, incoming):
    return norm_scale * (incoming - normed * jnp.mean(incoming * normed, axis=-1, keepdims=True))


def silu_slope(values):
    sigmoid_v = jax.nn.sigmoid(values)
    return sigmoid_v * (1.0 + values * (1.0 - sigmoid_v))


def build_decays(cumulative):
    per_head = jnp.transpose(cumulative, (0, 2, 1))
    rows_in = per_head.shape[2]
    causal = jnp.arange(rows_in)[:, None] >= jnp.arange(rows_in)[None, :]
    log_gaps = jnp.minimum(per_head[:, :, :, None] - per_head[:, :, None, :], 0.0)
    return jnp.where(causal, jnp.exp(log_gaps), 0.0)


def adamw_step(weight, first, second, gradient):
    first_new = BETA_ONE * first + (1.0 - BETA_ONE) * gradient
    second_new = BETA_TWO * second + (1.0 - BETA_TWO) * gradient * gradient
    fix_one = 1.0 - BETA_ONE**STEP
    fix_two = 1.0 - BETA_TWO**STEP
    update = first_new / fix_one / (jnp.sqrt(second_new / fix_two) + ADAM_EPS)
    return (weight - LEARN_RATE * (update + WEIGHT_DECAY * weight), first_new, second_new)


def mm(spec, a, b):
    return jnp.einsum(spec, a, b, preferred_element_type=f32)


def scatter_rows(value):
    return lax.psum_scatter(value.astype(bf16), "tp", scatter_dimension=0, tiled=True).astype(f32)


def gather_rows(value):
    return lax.all_gather(value, "tp", axis=0, tiled=True)


def solution(mesh):
    size = mesh.shape["seq"]

    def local(
        inputs,
        out_grad,
        seq_lengths,
        log_decay,
        mixer_weight,
        output_weight,
        glu_weight,
        down_weight,
        mixer_first,
        output_first,
        glu_first,
        down_first,
        mixer_second,
        output_second,
        glu_second,
        down_second,
    ):
        group_rows = log_decay.shape[0]
        heads_here = log_decay.shape[1]
        blocks_here = group_rows // BLK
        width_here = heads_here * HD
        ring = Ring(size)
        ring.place()
        seq_place = lax.axis_index("seq")
        keep_flags, token_mask = layout(seq_lengths, seq_place * blocks_here, blocks_here)
        mask_col = token_mask[:, None]
        mask_float = mask_col.astype(f32)

        mixer_low = mixer_weight.astype(bf16)
        output_low = output_weight.astype(bf16)
        glu_low = glu_weight.astype(bf16)
        down_low = down_weight.astype(bf16)

        inputs_f = inputs.astype(f32)
        normed_one, scale_one = normalize(inputs_f)
        rows_one = gather_rows(normed_one.astype(bf16))
        grad_rows = gather_rows(out_grad)

        key_full, value_full = in_turn(
            spread(ring, mixer_low[1], 0, 0), spread(ring, mixer_low[2], 0, 0)
        )
        query_full, gate_full = in_turn(
            spread(ring, mixer_low[0], 0, 0), spread(ring, mixer_low[3], 0, 0)
        )
        (output_full,) = in_turn(spread(ring, output_low, 1, 0))
        left_full, right_full = in_turn(
            spread(ring, glu_low[0], 0, 0), spread(ring, glu_low[1], 0, 0)
        )
        mid = down_low.shape[0] // 2
        down_parts = in_turn(
            spread(ring, down_low[:mid], 1, 0), spread(ring, down_low[mid:], 1, 0)
        )

        key_pre = mm("td,dc->tc", rows_one, key_full)
        value_pre = mm("td,dc->tc", rows_one, value_full)
        query_pre = mm("td,dc->tc", rows_one, query_full)
        gate_u = mm("td,dc->tc", rows_one, gate_full)
        zero_low = jnp.zeros((), bf16)
        queries = jax.nn.silu(query_pre).astype(bf16)
        keys_all = jnp.where(mask_col, jax.nn.silu(key_pre).astype(bf16), zero_low)
        values_all = jnp.where(mask_col, value_pre.astype(bf16), zero_low)
        block_shape = (blocks_here, BLK, heads_here, HD)
        query_blocks = queries.reshape(block_shape)
        key_blocks = keys_all.reshape(block_shape)
        value_blocks = values_all.reshape(block_shape)
        lower = (jnp.arange(BLK)[:, None] >= jnp.arange(BLK)[None, :]).astype(f32)
        cumulative = jnp.einsum(
            "ts,bsh->bth",
            lower,
            log_decay.reshape(blocks_here, BLK, heads_here),
            precision=lax.Precision.HIGHEST,
        )
        block_ends = cumulative[:, -1, :]
        exp_cum = jnp.exp(cumulative)[..., None]
        exp_tail = jnp.exp(block_ends[:, None, :] - cumulative)[..., None]
        decays = build_decays(cumulative)
        scaled_k = (key_blocks * exp_tail).astype(bf16)
        state_terms = mm("bshe,bshf->bhef", scaled_k, value_blocks)
        factors = keep_flags[:, None] * jnp.exp(block_ends)

        state = state_terms[0]
        factor = factors[0]
        for j in range(1, blocks_here):
            state = factors[j][:, None, None] * state + state_terms[j]
            factor = factor * factors[j]
        all_states = lax.all_gather(state.astype(bf16), "seq")
        all_factors = lax.all_gather(factor, "seq")
        place = jnp.arange(size)

        def reach(between):
            picked = jnp.where(between[:, :, None], all_factors[None, :, :], 1.0)
            total = picked[:, 0]
            for i in range(1, size):
                total = total * picked[:, i]
            return total

        from_before = jnp.where(
            (place < seq_place)[:, None],
            reach((place[None, :] > place[:, None]) & (place[None, :] < seq_place)),
            0.0,
        )
        from_after = jnp.where(
            (place > seq_place)[:, None],
            reach((place[None, :] < place[:, None]) & (place[None, :] > seq_place)),
            0.0,
        )
        entering = jnp.sum(from_before[:, :, None, None] * all_states.astype(f32), axis=0)
        used = []
        for j in range(blocks_here):
            used.append(keep_flags[j] * entering)
            entering = factors[j][:, None, None] * entering + state_terms[j]
        used_low = jnp.stack(used).astype(bf16)

        scores = mm("bthe,bshe->bhts", query_blocks, key_blocks)
        block_probs = (scores * decays).astype(bf16)
        inner_part = mm("bhts,bshf->bthf", block_probs, value_blocks)
        scaled_q = (query_blocks * exp_cum).astype(bf16)
        outer_part = mm("bthe,bhef->bthf", scaled_q, used_low)
        mixer_out = (inner_part + outer_part).reshape(group_rows, width_here)
        squares = lax.psum(jnp.sum(mixer_out * mixer_out, axis=1), "tp")
        mixer_scale = lax.rsqrt(squares / D + NORM_EPS)[:, None]
        mixer_normed = mixer_out * mixer_scale
        joined = (mixer_normed * gate_u).astype(bf16)
        branch = scatter_rows(mm("tc,cd->td", joined, output_full))
        middle = inputs_f + branch
        normed_two, scale_two = normalize(middle)
        rows_two = gather_rows(normed_two.astype(bf16))

        gate_left = mm("td,dc->tc", rows_two, left_full)
        gate_right = mm("td,dc->tc", rows_two, right_full)
        product = (gate_left * gate_right).astype(bf16)
        down_full = jnp.concatenate(down_parts, axis=0)
        product_grad = mm("td,cd->tc", grad_rows, down_full)
        left_grad = (product_grad * gate_right).astype(bf16)
        right_grad = (product_grad * gate_left).astype(bf16)
        two_grad = scatter_rows(
            mm("tc,dc->td", left_grad, left_full) + mm("tc,dc->td", right_grad, right_full)
        )
        middle_grad = out_grad.astype(f32) + norm_back(normed_two, scale_two, two_grad)
        branch_grad = gather_rows(middle_grad.astype(bf16))

        feed_in, _ = lax.optimization_barrier((product, branch_grad))
        feed_out = scatter_rows(mm("tc,cd->td", feed_in, down_full))
        block_out = (middle + feed_out).astype(bf16)

        def columns(rows, off):
            wide = rows.shape[1] // size
            return lax.dynamic_slice_in_dim(rows, ring.owner[off] * wide, wide, axis=1)

        down_sums = in_turn(
            collect(ring, lambda off: mm("tc,td->cd", product[:, :mid], columns(grad_rows, off)), 0),
            collect(ring, lambda off: mm("tc,td->cd", product[:, mid:], columns(grad_rows, off)), 0),
        )
        glu_sums = in_turn(
            collect(ring, lambda off: mm("td,tc->dc", columns(rows_two, off), left_grad), 0),
            collect(ring, lambda off: mm("td,tc->dc", columns(rows_two, off), right_grad), 0),
        )

        joined_grad = mm("td,cd->tc", branch_grad, output_full)
        gate_grad = (joined_grad * mixer_normed).astype(bf16)
        output_sum, gate_sum = in_turn(
            collect(ring, lambda off: mm("tc,td->cd", joined, columns(branch_grad, off)), 0),
            collect(ring, lambda off: mm("td,tc->dc", columns(rows_one, off), gate_grad), 0),
        )
        normed_grad = joined_grad * gate_u
        row_dots = lax.psum(jnp.sum(normed_grad * mixer_normed, axis=1), "tp")
        mixed_grad = (
            mixer_scale * (normed_grad - mixer_normed * (row_dots / D)[:, None])
        ).astype(bf16)
        grad_blocks = mixed_grad.reshape(block_shape)
        kept_terms = keep_flags[:, None, None, None] * mm("bthe,bthf->bhef", scaled_q, grad_blocks)
        back = kept_terms[blocks_here - 1]
        for j in range(blocks_here - 2, -1, -1):
            back = factors[j][:, None, None] * back + kept_terms[j]
        all_back = lax.all_gather(back.astype(bf16), "seq")
        leaving = jnp.sum(from_after[:, :, None, None] * all_back.astype(f32), axis=0)
        state_grads = [None] * blocks_here
        for j in range(blocks_here - 1, -1, -1):
            state_grads[j] = leaving
            leaving = factors[j][:, None, None] * leaving + kept_terms[j]
        state_low = jnp.stack(state_grads).astype(bf16)
        value_dots = mm("bthf,bshf->bhts", grad_blocks, value_blocks)
        score_grad = (value_dots * decays).astype(bf16)
        query_grad = (
            mm("bhts,bshe->bthe", score_grad, key_blocks)
            + mm("bthf,bhef->bthe", grad_blocks, used_low) * exp_cum
        )
        key_grad = (
            mm("bhts,bthe->bshe", score_grad, query_blocks)
            + mm("bshf,bhef->bshe", value_blocks, state_low) * exp_tail
        )
        value_grad = mm("bhts,bthf->bshf", block_probs, grad_blocks) + mm(
            "bshe,bhef->bshf", scaled_k, state_low
        )
        query_back = (query_grad.reshape(group_rows, width_here) * silu_slope(query_pre)).astype(
            bf16
        )
        key_back = (
            key_grad.reshape(group_rows, width_here) * mask_float * silu_slope(key_pre)
        ).astype(bf16)
        value_back = (value_grad.reshape(group_rows, width_here) * mask_float).astype(bf16)

        query_sum, key_sum, value_sum = in_turn(
            collect(ring, lambda off: mm("td,tc->dc", columns(rows_one, off), query_back), 0),
            collect(ring, lambda off: mm("td,tc->dc", columns(rows_one, off), key_back), 0),
            collect(ring, lambda off: mm("td,tc->dc", columns(rows_one, off), value_back), 0),
        )
        one_grad = scatter_rows(
            mm("tc,dc->td", query_back, query_full)
            + mm("tc,dc->td", key_back, key_full)
            + mm("tc,dc->td", value_back, value_full)
            + mm("tc,dc->td", gate_grad, gate_full)
        )
        input_grad = middle_grad + norm_back(normed_one, scale_one, one_grad)

        mixer_sum = jnp.stack([query_sum, key_sum, value_sum, gate_sum])
        glu_sum = jnp.stack(glu_sums)
        down_sum = jnp.concatenate(down_sums, axis=0)
        mixer_new, mixer_first_new, mixer_second_new = adamw_step(
            mixer_weight, mixer_first, mixer_second, mixer_sum
        )
        output_new, output_first_new, output_second_new = adamw_step(
            output_weight, output_first, output_second, output_sum
        )
        glu_new, glu_first_new, glu_second_new = adamw_step(
            glu_weight, glu_first, glu_second, glu_sum
        )
        down_new, down_first_new, down_second_new = adamw_step(
            down_weight, down_first, down_second, down_sum
        )
        return (
            block_out,
            input_grad,
            mixer_new,
            output_new,
            glu_new,
            down_new,
            mixer_first_new,
            output_first_new,
            glu_first_new,
            down_first_new,
            mixer_second_new,
            output_second_new,
            glu_second_new,
            down_second_new,
        )

    rows = P(("seq", "tp"), None)
    deep, tall = P(None, "seq", "tp"), P("tp", "seq")
    weights = (deep, tall, deep, tall)
    in_specs = (rows, rows, P(), P("seq", "tp"), *weights * 3)
    out_specs = (rows, rows, *weights * 3)
    return jax.shard_map(local, mesh=mesh, in_specs=in_specs, out_specs=out_specs, check_vma=False)
```

```python
import functools

import jax
import jax.numpy as jnp
from jax import lax
from jax.experimental import pallas as pl
from jax.experimental.pallas import tpu as pltpu
from jax.sharding import PartitionSpec as P

D = 2048
HD = 128
BLK = 256
STEP = 10


NORM_EPS = 1e-06
BETA_ONE = 0.9
BETA_TWO = 0.95
ADAM_EPS = 1e-08
WEIGHT_DECAY = 0.1
LEARN_RATE = 0.02

bf16 = jnp.bfloat16
f32 = jnp.float32


class Ring:
    def __init__(self, size):
        self.size = size
        self.half = size // 2
        self.order = [*range(0, size, 2), *range(size - 1, 0, -2)]
        after = {a: self.order[(i + 1) % size] for i, a in enumerate(self.order)}
        self.perms = ([(a, b) for a, b in after.items()], [(b, a) for a, b in after.items()])
        self.offsets = [0]
        for k in range(1, self.half):
            self.offsets += [-k, k]
        self.offsets.append(self.half)
        self.groups = []
        self.sent = []
        self.after = ()

    def place(self):
        size = self.size
        index = lax.axis_index("seq")
        here = jnp.where(index % 2 == 0, index // 2, size - 1 - index // 2)

        def device(spot):
            spot = lax.rem(spot + size, size)
            return jnp.where(spot < size // 2, 2 * spot, 2 * (size - 1 - spot) + 1)

        def rank(off):
            off = lax.rem(off + size, size)
            return jnp.where(off == 0, 0, jnp.where(off < size // 2, 2 * off, 2 * (size - off) - 1))

        self.into = [device(here + off) for off in self.offsets]
        spots = [a // 2 if a % 2 == 0 else size - 1 - a // 2 for a in range(size)]
        self.back = [rank(spot - here) for spot in spots]

    def pick(self, rows, places):
        wide = rows.shape[1] // self.size
        return jnp.concatenate(
            [lax.dynamic_slice_in_dim(rows, at * wide, wide, axis=1) for at in places], axis=1
        )

    def columns(self, rows, off):
        wide = rows.shape[1] // self.size
        at = self.offsets.index(off) * wide
        return rows[:, at : at + wide]

    def send(self, value, way):
        waits = [v for group in self.groups[-3:-1] for v in group]
        if waits or self.after:
            value = lax.optimization_barrier((value, *waits, *self.after))[0]
        self.sent.append(value)
        return lax.ppermute(value, "seq", self.perms[way])


def spread(ring, shard, side):
    pieces = [shard]
    ends = [shard, shard]
    for _ in range(1, ring.half):
        ends = [ring.send(end, way) for way, end in enumerate(ends)]
        pieces += ends
        yield ends
    far = ring.send(ends[side], side)
    pieces.append(far)
    yield [far]
    return pieces


def collect(ring, own, side):
    def add(parts, other):
        sums, at = [], 0
        for p in parts:
            sums.append(p + other[:, at : at + p.shape[1]].astype(f32))
            at += p.shape[1]
        return sums

    def low(parts):
        parts = [p.astype(bf16) for p in parts]
        return parts[0] if len(parts) == 1 else jnp.concatenate(parts, axis=1)

    ends = [None, None]
    ends[side] = ring.send(low(own(ring.half)), side)
    yield [ends[side]]
    for k in range(ring.half - 1, 0, -1):
        parts = [own(off) if end is None else add(own(off), end) for off, end in zip((k, -k), ends)]
        ends = [ring.send(low(p), way) for way, p in enumerate(parts)]
        yield ends
    return add(add(own(0), ends[0]), ends[1])


def turns(lanes, count, *after):
    for _ in range(count):
        for lane in lanes:
            lane.turn(*after)


def then(lanes, turn, *values):
    waits = [v for lane in lanes for v in lane.got[turn - 1]]
    out = lax.optimization_barrier((*values, *waits))[: len(values)]
    return out if len(values) > 1 else out[0]


def behind(lanes, turn, *values):
    waits = [v for lane in lanes for v in lane.gave[turn - 1]]
    out = lax.optimization_barrier((*values, *waits))[: len(values)]
    return out if len(values) > 1 else out[0]


class Line:
    def __init__(self, ring, work):
        self.ring = ring
        self.work = work
        self.got = []
        self.gave = []

    def turn(self, *after):
        self.ring.after = after
        before = len(self.ring.sent)
        self.got.append(next(self.work))
        self.ring.groups.append(self.got[-1])
        self.ring.after = ()
        self.gave.append(self.ring.sent[before:])

    def end(self):
        try:
            next(self.work)
        except StopIteration as end:
            return end.value
        raise ValueError("turns left")


def layout(seq_lengths, first_block, block_count):
    blocks = (seq_lengths + BLK - 1) // BLK
    count = seq_lengths.shape[0]
    earlier = jnp.arange(count)[:, None] > jnp.arange(count)[None, :]
    starts = jnp.sum(jnp.where(earlier, blocks[None, :], 0), axis=1)
    block_index = first_block + jnp.arange(block_count, dtype=jnp.int32)
    begins = starts[None, :] == block_index[:, None]
    keep_flags = 1.0 - jnp.any(begins, axis=1).astype(jnp.float32)
    owner_index = jnp.sum((starts[None, :] <= block_index[:, None]).astype(jnp.int32), axis=1) - 1
    chosen = jnp.arange(count, dtype=jnp.int32)[None, :] == owner_index[:, None]
    own_start = jnp.sum(jnp.where(chosen, starts[None, :], 0), axis=1)
    own_length = jnp.sum(jnp.where(chosen, seq_lengths[None, :], 0), axis=1)
    position = (block_index - own_start)[:, None] * BLK + jnp.arange(BLK, dtype=jnp.int32)[None, :]
    token_mask = position < own_length[:, None]
    return (keep_flags, token_mask.reshape(block_count * BLK))


def normalize(values):
    norm_scale = lax.rsqrt(jnp.mean(values * values, axis=-1, keepdims=True) + NORM_EPS)
    return (values * norm_scale, norm_scale)


def norm_back(normed, norm_scale, incoming):
    return norm_scale * (incoming - normed * jnp.mean(incoming * normed, axis=-1, keepdims=True))


MEBI = 2**20


def dot(a, b):
    return lax.dot_general(a, b, (((1,), (0,)), ((), ())), preferred_element_type=f32)


def dot_t(a, b):
    return lax.dot_general(a, b, (((1,), (1,)), ((), ())), preferred_element_type=f32)


def t_dot(a, b):
    return lax.dot_general(a, b, (((0,), (0,)), ((), ())), preferred_element_type=f32)


class Rows:
    def __init__(self, array):
        self.array = array


class Scalars:
    def __init__(self, array):
        self.array = array


def by_block(body, inputs, weights, outs, scratch=(), backward=False, vmem=60, flops=0):
    count = next(i.array.shape[0] for i in inputs if isinstance(i, Rows)) // BLK
    pieces = [p for stack in weights for group, _, _ in stack for p in group]
    turn = (lambda i: count - 1 - i) if backward else (lambda i: i)

    def spec(shape):
        part = shape[0] // count
        return pl.BlockSpec(
            (part, *shape[1:]), lambda i: (turn(i), *[0] * (len(shape) - 1))
        )

    def whole(shape):
        return pl.BlockSpec(shape, lambda i: (0,) * len(shape))

    in_specs, arrays = [], []
    for i in inputs:
        if isinstance(i, Rows):
            in_specs.append(spec(i.array.shape))
            arrays.append(i.array)
        elif isinstance(i, Scalars):
            in_specs.append(pl.BlockSpec(memory_space=pltpu.SMEM))
            arrays.append(i.array)
        else:
            in_specs.append(whole(i.shape))
            arrays.append(i)
    in_specs += [pl.BlockSpec(memory_space=pl.ANY)] * len(pieces)
    stacks = [
        (sum(p.shape[0] for p in stack[0][0]), sum(end - start for _, start, end in stack))
        for stack in weights
    ]

    def kernel(*refs):
        ins, refs = refs[: len(arrays)], refs[len(arrays) :]
        sources, refs = refs[: len(pieces)], refs[len(pieces) :]
        results, refs = refs[: len(outs)], refs[len(outs) :]
        held, refs = refs[: len(stacks)], refs[len(stacks) :]
        extra, sems = refs[: len(scratch)], refs[len(scratch) :]
        at = pl.program_id(0)

        if pieces:

            @pl.when(at == 0)
            def _():
                copies = []
                k = 0
                for parts, stack in zip(weights, held, strict=True):
                    column = 0
                    for group, start, end in parts:
                        row = 0
                        for p in group:
                            copies.append(
                                pltpu.make_async_copy(
                                    sources[k].at[:, start:end],
                                    stack.at[
                                        pl.ds(row, p.shape[0]), pl.ds(column, end - start)
                                    ],
                                    sems[0].at[k],
                                )
                            )
                            row += p.shape[0]
                            k += 1
                        column += end - start
                for c in copies:
                    c.start()
                for c in copies:
                    c.wait()

        body(at, turn(at), ins, held, results, extra)

    out = pl.pallas_call(
        kernel,
        grid=(count,),
        in_specs=in_specs,
        out_specs=[spec(shape) if cut else whole(shape) for shape, _, cut in outs],
        out_shape=[jax.ShapeDtypeStruct(shape, kind) for shape, kind, _ in outs],
        scratch_shapes=[
            *[pltpu.VMEM(shape, bf16) for shape in stacks],
            *scratch,
            *([pltpu.SemaphoreType.DMA((len(pieces),))] if pieces else []),
        ],
        compiler_params=pltpu.CompilerParams(
            dimension_semantics=("arbitrary",), vmem_limit_bytes=vmem * MEBI
        ),
        cost_estimate=pl.CostEstimate(
            flops=int(flops * COST), bytes_accessed=0, transcendentals=0
        ),
    )(*arrays, *pieces)
    return out


def enter(ring, inputs, out_grad):
    rows, width = inputs.shape
    wide = width // ring.size
    if wide % 128:
        here = ring.pick(inputs, ring.into)
        normed, scale = normalize(here.astype(f32))
        return normed.astype(bf16), here, ring.pick(out_grad, ring.into), scale

    def kernel(into, in_ref, grad_ref, normed_ref, here_ref, grad_here_ref, scale_ref):
        values = in_ref[...].astype(f32)
        scale = lax.rsqrt(jnp.mean(values * values, axis=-1, keepdims=True) + NORM_EPS)
        scale_ref[...] = scale
        for i in range(ring.size):
            at = pl.ds(pl.multiple_of(into[i] * wide, 128), wide)
            to = slice(i * wide, (i + 1) * wide)
            part = in_ref[:, at]
            here_ref[:, to] = part
            normed_ref[:, to] = (part.astype(f32) * scale).astype(bf16)
            grad_here_ref[:, to] = grad_ref[:, at]

    return pl.pallas_call(
        kernel,
        in_specs=[pl.BlockSpec(memory_space=pltpu.SMEM)] + [pl.BlockSpec(inputs.shape)] * 2,
        out_shape=[jax.ShapeDtypeStruct(inputs.shape, bf16)] * 3
        + [jax.ShapeDtypeStruct((rows, 1), f32)],
        compiler_params=pltpu.CompilerParams(vmem_limit_bytes=60 * MEBI),
    )(jnp.stack(ring.into), inputs, out_grad)


def leave(ring, kind, function, *values):
    rows, width = values[0].shape
    wide = width // ring.size
    if wide % 128:
        return ring.pick(function(*values).astype(kind), ring.back)

    def kernel(into, *refs):
        result = function(*[r[...] for r in refs[:-1]]).astype(kind)
        for i in range(ring.size):
            at = pl.ds(pl.multiple_of(into[i] * wide, 128), wide)
            refs[-1][:, at] = result[:, i * wide : (i + 1) * wide]

    return pl.pallas_call(
        kernel,
        in_specs=[pl.BlockSpec(memory_space=pltpu.SMEM)] + [pl.BlockSpec(v.shape) for v in values],
        out_shape=jax.ShapeDtypeStruct((rows, width), kind),
        compiler_params=pltpu.CompilerParams(vmem_limit_bytes=60 * MEBI),
    )(jnp.stack(ring.into), *values)


def head(ref, h):
    return ref[:, h * HD : (h + 1) * HD]


def decay_of(column, row):
    causal = lax.broadcasted_iota(jnp.int32, (BLK, BLK), 0) >= lax.broadcasted_iota(
        jnp.int32, (BLK, BLK), 1
    )
    return jnp.where(causal, jnp.exp(jnp.minimum(column - row, 0.0)), 0.0)


def silu_slope(values):
    sigmoid_v = jax.nn.sigmoid(values)
    return sigmoid_v * (1.0 + values * (1.0 - sigmoid_v))


def keys_kernel(heads, at, block, ins, held, outs, extra):
    rows, mask, tail, factors, ending = ins
    pre_out, keys_out, values_out, scaled_out, terms_out, message_out = outs
    (state,) = extra
    wide = heads * HD

    @pl.when(at == 0)
    def _():
        state[...] = jnp.zeros_like(state)
        message_out[wide:, :] = ending[...]

    pre = dot(rows[...], held[0][...])
    key_pre, value_pre = pre[:, :wide], pre[:, wide:]
    pre_out[...] = key_pre
    keep = mask[...]
    keys = (jax.nn.silu(key_pre).astype(bf16) * keep).astype(bf16)
    values = (value_pre.astype(bf16) * keep).astype(bf16)
    keys_out[...] = keys
    values_out[...] = values
    for h in range(heads):
        part = slice(h * HD, (h + 1) * HD)
        scaled = (keys[:, part].astype(f32) * tail[:, h : h + 1]).astype(bf16)
        scaled_out[:, part] = scaled
        term = t_dot(scaled, values[:, part])
        terms_out[part, :] = term
        renewed = factors[block, h] * state[part, :] + term
        state[part, :] = renewed
        message_out[part, :] = renewed.astype(bf16)


def queries_kernel(heads, at, block, ins, held, outs, extra):
    rows, keys, values, column, row = ins
    pre_out, gate_out, queries_out, scaled_out, probs_out, inner_out = outs
    wide = heads * HD
    both = dot(rows[...], held[0][...])
    query_pre = both[:, :wide]
    pre_out[...] = query_pre
    gate_out[...] = both[:, wide:]
    queries = jax.nn.silu(query_pre).astype(bf16)
    queries_out[...] = queries
    for h in range(heads):
        here = queries[:, h * HD : (h + 1) * HD]
        sums = column[:, h : h + 1]
        scaled_out[:, h * HD : (h + 1) * HD] = (here.astype(f32) * jnp.exp(sums)).astype(bf16)
        decays = decay_of(sums, row[0, h : h + 1, :])
        probs = (dot_t(here, head(keys, h)) * decays).astype(bf16)
        probs_out[:, h * BLK : (h + 1) * BLK] = probs
        inner_out[:, h * HD : (h + 1) * HD] = dot(probs, head(values, h))


def lanes(values):
    total = values[:, :HD]
    for i in range(1, values.shape[1] // HD):
        total = total + values[:, i * HD : (i + 1) * HD]
    return total


def states_kernel(heads, at, block, ins, held, outs, extra):
    inner, scaled, terms, message, reach, factors, keep = ins
    mixed_out, squares_out, used_out = outs
    (state,) = extra
    size = reach.shape[0]

    @pl.when(at == 0)
    def _():
        for h in range(heads):
            total = reach[0, h] * message[0, h * HD : (h + 1) * HD, :].astype(f32)
            for i in range(1, size):
                total = total + reach[i, h] * message[i, h * HD : (h + 1) * HD, :].astype(f32)
            state[h * HD : (h + 1) * HD, :] = total

    parts = []
    for h in range(heads):
        now = state[h * HD : (h + 1) * HD, :]
        used = (keep[block] * now).astype(bf16)
        used_out[h * HD : (h + 1) * HD, :] = used
        state[h * HD : (h + 1) * HD, :] = factors[block, h] * now + terms[h * HD : (h + 1) * HD, :]
        parts.append(head(inner, h) + dot(head(scaled, h), used))
    mixed = jnp.concatenate(parts, axis=1)
    mixed_out[...] = mixed
    squares_out[...] = lanes(mixed * mixed)


def branch_kernel(at, block, ins, held, outs, extra):
    mixed, gate, scale = ins
    joined_out, branch_out = outs
    joined = (mixed[...] * scale[...] * gate[...]).astype(bf16)
    joined_out[...] = joined
    branch_out[...] = dot_t(joined, held[0][...]).astype(bf16)


def gates_kernel(at, block, ins, held, outs, extra):
    (rows,) = ins
    left_out, right_out, product_out = outs
    hidden = left_out.shape[1]
    gates = dot(rows[...], held[0][...])
    left, right = gates[:, :hidden], gates[:, hidden:]
    left_out[...] = left
    right_out[...] = right
    product_out[...] = (left * right).astype(bf16)


def gates_back_kernel(at, block, ins, held, outs, extra):
    rows, left, right = ins
    (both_out,) = outs
    hidden = left.shape[1]
    product_grad = dot(rows[...], held[0][...])
    both_out[:, :hidden] = (product_grad * right[...]).astype(bf16)
    both_out[:, hidden:] = (product_grad * left[...]).astype(bf16)


def back_kernel(at, block, ins, held, outs, extra):
    total = dot_t(ins[0][...], held[0][...])
    for i, stack in zip(ins[1:], held[1:], strict=True):
        total = total + dot_t(i[...], stack[...])
    outs[0][...] = total.astype(bf16)


def joined_back_kernel(at, block, ins, held, outs, extra):
    rows, mixed, gate, scale = ins
    gate_out, inward_out, dots_out = outs
    joined_grad = dot(rows[...], held[0][...])
    normed = mixed[...] * scale[...]
    gate_out[...] = (joined_grad * normed).astype(bf16)
    inward = joined_grad * gate[...]
    inward_out[...] = inward
    dots_out[...] = lanes(inward * normed)


def mixed_back_kernel(heads, at, block, ins, held, outs, extra):
    inward, mixed, scale, dots, scaled, factors, keep = ins
    grad_out, kept_out, back_out = outs
    (state,) = extra
    normed = mixed[...] * scale[...]
    grad = (scale[...] * (inward[...] - normed * dots[...])).astype(bf16)
    grad_out[...] = grad

    @pl.when(at == 0)
    def _():
        state[...] = jnp.zeros_like(state)

    for h in range(heads):
        part = slice(h * HD, (h + 1) * HD)
        kept = keep[block] * t_dot(head(scaled, h), grad[:, part])
        kept_out[part, :] = kept
        renewed = factors[block, h] * state[part, :] + kept
        state[part, :] = renewed
        back_out[part, :] = renewed.astype(bf16)


def scores_back_kernel(heads, at, block, ins, held, outs, extra):
    grad, keys, values, queries, probs, used, query_pre, column, row = ins
    query_out, key_out, value_out = outs
    for h in range(heads):
        part = slice(h * HD, (h + 1) * HD)
        here = grad[:, part]
        sums = column[:, h : h + 1]
        score = (dot_t(here, values[:, part]) * decay_of(sums, row[0, h : h + 1, :])).astype(bf16)
        query_grad = dot(score, keys[:, part]) + dot_t(here, used[part, :]) * jnp.exp(sums)
        query_out[:, part] = (query_grad * silu_slope(query_pre[:, part])).astype(bf16)
        key_out[:, part] = t_dot(score, queries[:, part])
        value_out[:, part] = t_dot(probs[:, h * BLK : (h + 1) * BLK], here)


def states_back_kernel(heads, at, block, ins, held, outs, extra):
    key_grad, value_grad, query, gate, values, scaled, kept, message = ins[:8]
    key_pre, mask, tail, reach, factors = ins[8:]
    pair_out, other_out = outs
    (state,) = extra
    size = reach.shape[0]
    wide = heads * HD

    @pl.when(at == 0)
    def _():
        for h in range(heads):
            total = reach[0, h] * message[0, h * HD : (h + 1) * HD, :].astype(f32)
            for i in range(1, size):
                total = total + reach[i, h] * message[i, h * HD : (h + 1) * HD, :].astype(f32)
            state[h * HD : (h + 1) * HD, :] = total

    keep = mask[...]
    for h in range(heads):
        part = slice(h * HD, (h + 1) * HD)
        now = state[part, :]
        low = now.astype(bf16)
        key = key_grad[:, part] + dot_t(values[:, part], low) * tail[:, h : h + 1]
        pair_out[:, part] = (key * keep * silu_slope(key_pre[:, part])).astype(bf16)
        value = value_grad[:, part] + dot(scaled[:, part], low)
        pair_out[:, wide + h * HD : wide + (h + 1) * HD] = (value * keep).astype(bf16)
        state[part, :] = factors[block, h] * now + kept[part, :]
    other_out[:, :wide] = query[...]
    other_out[:, wide:] = gate[...]


COST = 0.0


def mm(spec, a, b):
    return jnp.einsum(spec, a, b, preferred_element_type=f32)


def scatter_rows(value):
    return lax.psum_scatter(value, "tp", scatter_dimension=0, tiled=True)


def gather_rows(value):
    return lax.all_gather(value, "tp", axis=0, tiled=True)


def adamw_step(weight, first, second, gradient):
    first_new = BETA_ONE * first + (1.0 - BETA_ONE) * gradient
    second_new = BETA_TWO * second + (1.0 - BETA_TWO) * gradient * gradient
    fix_one = 1.0 - BETA_ONE**STEP
    fix_two = 1.0 - BETA_TWO**STEP
    update = first_new / fix_one / (jnp.sqrt(second_new / fix_two) + ADAM_EPS)
    return (weight - LEARN_RATE * (update + WEIGHT_DECAY * weight), first_new, second_new)


def adamw_across(weight, first, second, gradient):
    rows, columns = weight.shape
    part = 128

    def kernel(w, m, v, g, w_out, m_out, v_out):
        results = adamw_step(w[...], m[...], v[...], g[...].T)
        for ref, value in zip((w_out, m_out, v_out), results, strict=True):
            ref[...] = value

    here = pl.BlockSpec((part, columns), lambda i: (i, 0))
    return pl.pallas_call(
        kernel,
        grid=(rows // part,),
        in_specs=[here] * 3 + [pl.BlockSpec((columns, part), lambda i: (0, i))],
        out_specs=[here] * 3,
        out_shape=[jax.ShapeDtypeStruct(weight.shape, f32)] * 3,
        compiler_params=pltpu.CompilerParams(vmem_limit_bytes=60 * MEBI),
    )(weight, first, second, gradient)


def solution(mesh):
    size = mesh.shape["seq"]

    def local(
        inputs,
        out_grad,
        seq_lengths,
        log_decay,
        mixer_weight,
        output_weight,
        glu_weight,
        down_weight,
        mixer_first,
        output_first,
        glu_first,
        down_first,
        mixer_second,
        output_second,
        glu_second,
        down_second,
    ):
        rows = log_decay.shape[0]
        heads = log_decay.shape[1]
        blocks = rows // BLK
        wide = heads * HD
        hidden = down_weight.shape[0]
        ring = Ring(size)
        ring.place()
        half = ring.half
        seq_place = lax.axis_index("seq")
        keep_flags, token_mask = layout(seq_lengths, seq_place * blocks, blocks)
        mask_col = token_mask[:, None].astype(f32)

        output_low = output_weight.astype(bf16).T
        down_low = down_weight.astype(bf16).T
        pair, part = 2 * wide, wide // 2
        cut = hidden // 256 * 128
        mixer_lanes = [
            jnp.concatenate(
                [mixer_weight[i].astype(bf16), mixer_weight[j].astype(bf16), output_low[:, a:b]], axis=1
            )
            for i, j, a, b in ((1, 2, 0, part), (0, 3, part, wide))
        ]
        mixer = [Line(ring, spread(ring, low, i)) for i, low in enumerate(mixer_lanes)]
        glu = [Line(ring, spread(ring, glu_weight[i].astype(bf16), i)) for i in range(2)]
        down = [
            Line(ring, spread(ring, low, i))
            for i, low in enumerate((down_low[:, :cut], down_low[:, cut:]))
        ]

        rows_one_here, inputs_here, out_grad_here, scale_one = enter(ring, inputs, out_grad)
        rows_one = gather_rows(rows_one_here)
        grad_rows = gather_rows(out_grad_here)

        lower = (jnp.arange(BLK)[:, None] >= jnp.arange(BLK)[None, :]).astype(f32)
        cumulative = jnp.einsum(
            "ts,bsh->bth",
            lower,
            log_decay.reshape(blocks, BLK, heads),
            precision=lax.Precision.HIGHEST,
        )
        block_ends = cumulative[:, -1, :]
        tail = jnp.exp(block_ends[:, None, :] - cumulative).reshape(rows, heads)
        column = cumulative.reshape(rows, heads)
        row = jnp.transpose(cumulative, (0, 2, 1))
        factors = keep_flags[:, None] * jnp.exp(block_ends)

        turns(mixer, half)
        mixer_full = [lane.end() for lane in mixer]
        pair_stack, other_stack = [[(full, 0, pair)] for full in mixer_full]
        output_stack = [(full, pair, pair + part) for full in mixer_full]
        turns(glu, half)
        turns(down, half - 1)

        state_shape = (blocks * wide, HD)
        factor = factors[0]
        for j in range(1, blocks):
            factor = factor * factors[j]
        first = factor.astype(bf16)
        second = (factor - first.astype(f32)).astype(bf16)
        third = (factor - first.astype(f32) - second.astype(f32)).astype(bf16)
        ending = jnp.pad(jnp.stack([first, second, third]), ((0, 13), (0, HD - heads)))
        key_pre, keys, values, scaled_k, terms, message = by_block(
            functools.partial(keys_kernel, heads),
            [
                Rows(then(mixer, half, rows_one)),
                Rows(mask_col),
                Rows(tail),
                Scalars(factors),
                ending,
            ],
            [pair_stack],
            [
                ((rows, wide), f32, True),
                ((rows, wide), bf16, True),
                ((rows, wide), bf16, True),
                ((rows, wide), bf16, True),
                (state_shape, f32, True),
                ((wide + 16, HD), bf16, False),
            ],
            [pltpu.VMEM((wide, HD), f32)],
            flops=2 * rows * D * 2 * wide,
        )
        message, grad_rows = then(glu[:1], 1, message, grad_rows)
        message = lax.all_gather(message, "seq")
        all_factors = jnp.sum(message[:, wide : wide + 3, :heads].astype(f32), axis=1)
        place = jnp.arange(size)

        def reach(between):
            picked = jnp.where(between[:, :, None], all_factors[None, :, :], 1.0)
            total = picked[:, 0]
            for i in range(1, size):
                total = total * picked[:, i]
            return total

        from_before = jnp.where(
            (place < seq_place)[:, None],
            reach((place[None, :] > place[:, None]) & (place[None, :] < seq_place)),
            0.0,
        )
        from_after = jnp.where(
            (place > seq_place)[:, None],
            reach((place[None, :] < place[:, None]) & (place[None, :] > seq_place)),
            0.0,
        )
        query_pre, gate_u, queries, scaled_q, probs, inner = by_block(
            functools.partial(queries_kernel, heads),
            [Rows(rows_one), Rows(keys), Rows(values), Rows(column), Rows(row)],
            [other_stack],
            [
                ((rows, wide), f32, True),
                ((rows, wide), f32, True),
                ((rows, wide), bf16, True),
                ((rows, wide), bf16, True),
                ((rows, heads * BLK), bf16, True),
                ((rows, wide), f32, True),
            ],
            flops=2 * rows * D * 2 * wide,
        )
        inner = then(glu[1:], 1, inner)
        message = then(glu[:1], 2, message)
        mixer_out, squares, used = by_block(
            functools.partial(states_kernel, heads),
            [
                Rows(inner),
                Rows(scaled_q),
                Rows(terms),
                message,
                Scalars(from_before),
                Scalars(factors),
                Scalars(keep_flags),
            ],
            [],
            [((rows, wide), f32, True), ((rows, HD), f32, True), (state_shape, bf16, True)],
            [pltpu.VMEM((wide, HD), f32)],
            flops=2 * rows * D * wide // 4,
        )
        squares = then(glu[1:], 2, squares)
        squares = lax.psum(jnp.sum(squares, axis=1), "tp")
        mixer_scale = lax.rsqrt(squares / D + NORM_EPS)[:, None]
        joined, branch_here = by_block(
            branch_kernel,
            [Rows(mixer_out), Rows(gate_u), Rows(mixer_scale)],
            [output_stack],
            [((rows, wide), bf16, True), ((rows, D), bf16, True)],
            flops=2 * rows * D * wide,
        )
        branch = scatter_rows(then(glu[:1], 3, branch_here))
        middle = inputs_here.astype(f32) + then(glu, half, branch).astype(f32)
        normed_two, scale_two = normalize(middle)
        rows_two_here = normed_two.astype(bf16)
        rows_two = gather_rows(rows_two_here)
        rows_two = then(down, 1, rows_two)

        glu_stack = [(lane.end(), 0, hidden) for lane in glu]
        gate_left, gate_right, product = by_block(
            gates_kernel,
            [Rows(rows_two)],
            [glu_stack],
            [((rows, hidden), f32, True), ((rows, hidden), f32, True), ((rows, hidden), bf16, True)],
            flops=2 * rows * D * 2 * hidden,
        )

        product = then(down, half - 1, product)
        turns(down, 1)
        down_parts = [lane.end() for lane in down]
        down_stack = [(full, 0, full[0].shape[1]) for full in down_parts]
        down_total = [
            Line(
                ring,
                collect(
                    ring,
                    lambda off, cols=cols: [mm("td,tc->dc", ring.columns(grad_rows, off), cols)],
                    i,
                ),
            )
            for i, cols in enumerate((product[:, :cut], product[:, cut:]))
        ]
        turns(down_total, 1)
        (both_grads,) = by_block(
            gates_back_kernel,
            [Rows(grad_rows), Rows(gate_left), Rows(gate_right)],
            [down_stack],
            [((rows, 2 * hidden), bf16, True)],
            flops=2 * rows * D * hidden,
        )
        both_grads = then(down_total, 1, both_grads)
        turns(down_total, 1)
        glu_total = [
            Line(
                ring,
                collect(
                    ring,
                    lambda off, cols=cols: [mm("td,tc->dc", ring.columns(rows_two, off), cols)],
                    i,
                ),
            )
            for i, cols in enumerate((both_grads[:, :hidden], both_grads[:, hidden:]))
        ]
        turns(glu_total, 1)
        (two_here,) = by_block(
            back_kernel,
            [Rows(behind(glu_total, 1, both_grads))],
            [glu_stack],
            [((rows, D), bf16, True)],
            flops=2 * rows * D * 2 * hidden,
        )
        two_grad = scatter_rows(then(down_total, 2, two_here))
        turns(down_total, half - 2)
        two_grad = behind(down_total, half, then(down_total, half - 1, two_grad))
        middle_grad = out_grad_here.astype(f32) + norm_back(
            normed_two, scale_two, two_grad.astype(f32)
        )
        branch_grad = gather_rows(middle_grad.astype(bf16))
        turns(glu_total, 1)
        branch_grad = then(glu_total[:1], 2, branch_grad)

        gate_grad, inward, dots = by_block(
            joined_back_kernel,
            [Rows(branch_grad), Rows(mixer_out), Rows(gate_u), Rows(mixer_scale)],
            [output_stack],
            [((rows, wide), bf16, True), ((rows, wide), f32, True), ((rows, HD), f32, True)],
            flops=2 * rows * D * wide,
        )
        turns(glu_total, half - 2)
        dots = then(glu_total[1:], 2, dots)
        row_dots = (lax.psum(jnp.sum(dots, axis=1), "tp") / D)[:, None]
        mixed_grad, kept, back = by_block(
            functools.partial(mixed_back_kernel, heads),
            [
                Rows(inward),
                Rows(mixer_out),
                Rows(mixer_scale),
                Rows(row_dots),
                Rows(scaled_q),
                Scalars(factors),
                Scalars(keep_flags),
            ],
            [],
            [((rows, wide), bf16, True), (state_shape, f32, True), ((wide, HD), bf16, False)],
            [pltpu.VMEM((wide, HD), f32)],
            backward=True,
            flops=2 * rows * D * wide // 4,
        )
        all_back = lax.all_gather(back, "seq")
        (feed_here,) = by_block(
            back_kernel,
            [Rows(lax.optimization_barrier((product, back))[0])],
            [down_stack],
            [((rows, D), bf16, True)],
            flops=2 * rows * D * hidden,
        )
        feed_here = then(glu_total[:1], 3, feed_here)
        query_back, key_grad, value_grad = by_block(
            functools.partial(scores_back_kernel, heads),
            [
                Rows(lax.optimization_barrier((mixed_grad, feed_here))[0]),
                Rows(keys),
                Rows(values),
                Rows(queries),
                Rows(probs),
                Rows(used),
                Rows(query_pre),
                Rows(column),
                Rows(row),
            ],
            [],
            [((rows, wide), bf16, True), ((rows, wide), f32, True), ((rows, wide), f32, True)],
            flops=2 * rows * D * wide,
        )
        query_back = then(glu_total[1:], 3, query_back)
        feed_out = scatter_rows(lax.optimization_barrier((feed_here, all_back))[0])
        pair_grads, other_grads = by_block(
            functools.partial(states_back_kernel, heads),
            [
                Rows(key_grad),
                Rows(value_grad),
                Rows(query_back),
                Rows(gate_grad),
                Rows(values),
                Rows(scaled_k),
                Rows(kept),
                then(glu_total[:1], half, all_back),
                Rows(key_pre),
                Rows(mask_col),
                Rows(tail),
                Scalars(from_after),
                Scalars(factors),
            ],
            [],
            [((rows, pair), bf16, True), ((rows, pair), bf16, True)],
            [pltpu.VMEM((wide, HD), f32)],
            backward=True,
            flops=2 * rows * D * wide // 4,
        )
        pair_grads, other_grads = then(glu_total, half, pair_grads, other_grads)
        mixer_total = [
            Line(
                ring,
                collect(
                    ring,
                    lambda off, grads=grads, cols=cols: [
                        mm("td,tc->dc", ring.columns(rows_one, off), grads),
                        mm("td,tc->dc", ring.columns(branch_grad, off), cols),
                    ],
                    i,
                ),
            )
            for i, (grads, cols) in enumerate(
                ((pair_grads, joined[:, :part]), (other_grads, joined[:, part:]))
            )
        ]
        turns(mixer_total, half - 1)
        block_out = leave(ring, bf16, lambda a, b: a + b.astype(f32), middle, feed_out)
        (one_here,) = by_block(
            back_kernel,
            [Rows(behind(mixer_total, 1, pair_grads)), Rows(other_grads)],
            [pair_stack, other_stack],
            [((rows, D), bf16, True)],
            flops=2 * rows * D * 4 * wide,
        )
        one_grad = scatter_rows(then(mixer_total, 1, one_here))
        one_grad = then(mixer_total, half - 1, one_grad)
        input_grad = leave(
            ring,
            f32,
            lambda grad, rows, scale, incoming: (
                grad + norm_back(rows.astype(f32) * scale, scale, incoming.astype(f32))
            ),
            middle_grad,
            inputs_here,
            scale_one,
            one_grad,
        )

        turns(mixer_total, 1, block_out, input_grad)
        down_sum = jnp.concatenate([lane.end()[0] for lane in down_total], axis=1)
        glu_sum = jnp.stack([lane.end()[0] for lane in glu_total])
        (pair_sum, first_sum), (other_sum, second_sum) = [lane.end() for lane in mixer_total]
        output_sum = jnp.concatenate([first_sum, second_sum], axis=1)

        mixer_sum = jnp.stack(
            [other_sum[:, :wide], pair_sum[:, :wide], pair_sum[:, wide:], other_sum[:, wide:]]
        )
        mixer_new, mixer_first_new, mixer_second_new = adamw_step(
            mixer_weight, mixer_first, mixer_second, mixer_sum
        )
        output_new, output_first_new, output_second_new = adamw_across(
            output_weight, output_first, output_second, output_sum
        )
        glu_new, glu_first_new, glu_second_new = adamw_step(
            glu_weight, glu_first, glu_second, then(mixer_total, 2, glu_sum)
        )
        down_new, down_first_new, down_second_new = adamw_across(
            down_weight, down_first, down_second, then(mixer_total, 1, down_sum)
        )
        return (
            block_out,
            input_grad,
            mixer_new,
            output_new,
            glu_new,
            down_new,
            mixer_first_new,
            output_first_new,
            glu_first_new,
            down_first_new,
            mixer_second_new,
            output_second_new,
            glu_second_new,
            down_second_new,
        )

    rows = P(("seq", "tp"), None)
    deep, tall = P(None, "seq", "tp"), P("tp", "seq")
    weights = (deep, tall, deep, tall)
    in_specs = (rows, rows, P(), P("seq", "tp"), *weights * 3)
    out_specs = (rows, rows, *weights * 3)
    return jax.shard_map(local, mesh=mesh, in_specs=in_specs, out_specs=out_specs, check_vma=False)
```

```python
import functools

import jax
import jax.numpy as jnp
from jax import lax
from jax.experimental import pallas as pl
from jax.experimental.pallas import tpu as pltpu
from jax.sharding import PartitionSpec as P

D = 2048
HD = 128
BLK = 256
STEP = 10


NORM_EPS = 1e-06
BETA_ONE = 0.9
BETA_TWO = 0.95
ADAM_EPS = 1e-08
WEIGHT_DECAY = 0.1
LEARN_RATE = 0.02

bf16 = jnp.bfloat16
f32 = jnp.float32


class Ring:
    def __init__(self, size):
        self.size = size
        self.half = size // 2
        self.order = [*range(0, size, 2), *range(size - 1, 0, -2)]
        after = {a: self.order[(i + 1) % size] for i, a in enumerate(self.order)}
        self.perms = ([(a, b) for a, b in after.items()], [(b, a) for a, b in after.items()])
        self.offsets = [0]
        for k in range(1, self.half):
            self.offsets += [-k, k]
        self.offsets.append(self.half)
        self.groups = []
        self.sent = []
        self.after = ()

    def place(self):
        size = self.size
        index = lax.axis_index("seq")
        here = jnp.where(index % 2 == 0, index // 2, size - 1 - index // 2)

        def device(spot):
            spot = lax.rem(spot + size, size)
            return jnp.where(spot < size // 2, 2 * spot, 2 * (size - 1 - spot) + 1)

        def rank(off):
            off = lax.rem(off + size, size)
            return jnp.where(off == 0, 0, jnp.where(off < size // 2, 2 * off, 2 * (size - off) - 1))

        self.into = [device(here + off) for off in self.offsets]
        spots = [a // 2 if a % 2 == 0 else size - 1 - a // 2 for a in range(size)]
        self.back = [rank(spot - here) for spot in spots]

    def pick(self, rows, places):
        wide = rows.shape[1] // self.size
        return jnp.concatenate(
            [lax.dynamic_slice_in_dim(rows, at * wide, wide, axis=1) for at in places], axis=1
        )

    def columns(self, rows, off):
        wide = rows.shape[1] // self.size
        at = self.offsets.index(off) * wide
        return rows[:, at : at + wide]

    def send(self, value, way):
        waits = [v for group in self.groups[-3:-1] for v in group]
        if waits or self.after:
            value = lax.optimization_barrier((value, *waits, *self.after))[0]
        self.sent.append(value)
        return lax.ppermute(value, "seq", self.perms[way])


def spread(ring, shard, side):
    pieces = [shard]
    ends = [shard, shard]
    for _ in range(1, ring.half):
        ends = [ring.send(end, way) for way, end in enumerate(ends)]
        pieces += ends
        yield ends
    far = ring.send(ends[side], side)
    pieces.append(far)
    yield [far]
    return pieces


def collect(ring, own, side):
    def add(parts, other):
        sums, at = [], 0
        for p in parts:
            sums.append(p + other[:, at : at + p.shape[1]].astype(f32))
            at += p.shape[1]
        return sums

    def low(parts):
        parts = [p.astype(bf16) for p in parts]
        return parts[0] if len(parts) == 1 else jnp.concatenate(parts, axis=1)

    ends = [None, None]
    ends[side] = ring.send(low(own(ring.half)), side)
    yield [ends[side]]
    for k in range(ring.half - 1, 0, -1):
        parts = [own(off) if end is None else add(own(off), end) for off, end in zip((k, -k), ends)]
        ends = [ring.send(low(p), way) for way, p in enumerate(parts)]
        yield ends
    return add(add(own(0), ends[0]), ends[1])


def turns(lanes, count, *after):
    for _ in range(count):
        for lane in lanes:
            lane.turn(*after)
        groups = lanes[0].ring.groups
        if len(lanes) == 2 and len(groups[-1]) == len(groups[-2]) == 1:
            groups[-2:] = [groups[-2] + groups[-1]]


def then(lanes, turn, *values):
    if turn < 1:
        return values if len(values) > 1 else values[0]
    waits = [v for lane in lanes for v in lane.got[turn - 1]]
    out = lax.optimization_barrier((*values, *waits))[: len(values)]
    return out if len(values) > 1 else out[0]


def behind(lanes, turn, *values):
    if turn < 1:
        return values if len(values) > 1 else values[0]
    waits = [v for lane in lanes for v in lane.gave[turn - 1]]
    out = lax.optimization_barrier((*values, *waits))[: len(values)]
    return out if len(values) > 1 else out[0]


class Line:
    def __init__(self, ring, work):
        self.ring = ring
        self.work = work
        self.got = []
        self.gave = []

    def turn(self, *after):
        self.ring.after = after
        before = len(self.ring.sent)
        self.got.append(next(self.work))
        self.ring.groups.append(self.got[-1])
        self.ring.after = ()
        self.gave.append(self.ring.sent[before:])

    def end(self):
        try:
            next(self.work)
        except StopIteration as end:
            return end.value
        raise ValueError("turns left")


def layout(seq_lengths, first_block, block_count):
    blocks = (seq_lengths + BLK - 1) // BLK
    count = seq_lengths.shape[0]
    earlier = jnp.arange(count)[:, None] > jnp.arange(count)[None, :]
    starts = jnp.sum(jnp.where(earlier, blocks[None, :], 0), axis=1)
    block_index = first_block + jnp.arange(block_count, dtype=jnp.int32)
    begins = starts[None, :] == block_index[:, None]
    keep_flags = 1.0 - jnp.any(begins, axis=1).astype(jnp.float32)
    owner_index = jnp.sum((starts[None, :] <= block_index[:, None]).astype(jnp.int32), axis=1) - 1
    chosen = jnp.arange(count, dtype=jnp.int32)[None, :] == owner_index[:, None]
    own_start = jnp.sum(jnp.where(chosen, starts[None, :], 0), axis=1)
    own_length = jnp.sum(jnp.where(chosen, seq_lengths[None, :], 0), axis=1)
    position = (block_index - own_start)[:, None] * BLK + jnp.arange(BLK, dtype=jnp.int32)[None, :]
    token_mask = position < own_length[:, None]
    return (keep_flags, token_mask.reshape(block_count * BLK))


def normalize(values):
    norm_scale = lax.rsqrt(jnp.mean(values * values, axis=-1, keepdims=True) + NORM_EPS)
    return (values * norm_scale, norm_scale)


def norm_back(normed, norm_scale, incoming):
    return norm_scale * (incoming - normed * jnp.mean(incoming * normed, axis=-1, keepdims=True))


MEBI = 2**20


def dot(a, b):
    return lax.dot_general(a, b, (((1,), (0,)), ((), ())), preferred_element_type=f32)


def dot_t(a, b):
    return lax.dot_general(a, b, (((1,), (1,)), ((), ())), preferred_element_type=f32)


def t_dot(a, b):
    return lax.dot_general(a, b, (((0,), (0,)), ((), ())), preferred_element_type=f32)


class Rows:
    def __init__(self, array):
        self.array = array


class Scalars:
    def __init__(self, array):
        self.array = array


def by_block(body, inputs, weights, outs, scratch=(), backward=False, vmem=60, flops=0):
    count = next(i.array.shape[0] for i in inputs if isinstance(i, Rows)) // BLK
    pieces = [p for stack in weights for group, _, _ in stack for p in group]
    turn = (lambda i: count - 1 - i) if backward else (lambda i: i)

    def spec(shape):
        part = shape[0] // count
        return pl.BlockSpec(
            (part, *shape[1:]), lambda i: (turn(i), *[0] * (len(shape) - 1))
        )

    def whole(shape):
        return pl.BlockSpec(shape, lambda i: (0,) * len(shape))

    in_specs, arrays = [], []
    for i in inputs:
        if isinstance(i, Rows):
            in_specs.append(spec(i.array.shape))
            arrays.append(i.array)
        elif isinstance(i, Scalars):
            in_specs.append(pl.BlockSpec(memory_space=pltpu.SMEM))
            arrays.append(i.array)
        else:
            in_specs.append(whole(i.shape))
            arrays.append(i)
    in_specs += [pl.BlockSpec(memory_space=pl.ANY)] * len(pieces)
    stacks = [
        (sum(p.shape[0] for p in stack[0][0]), sum(end - start for _, start, end in stack))
        for stack in weights
    ]

    def kernel(*refs):
        ins, refs = refs[: len(arrays)], refs[len(arrays) :]
        sources, refs = refs[: len(pieces)], refs[len(pieces) :]
        results, refs = refs[: len(outs)], refs[len(outs) :]
        held, refs = refs[: len(stacks)], refs[len(stacks) :]
        extra, sems = refs[: len(scratch)], refs[len(scratch) :]
        at = pl.program_id(0)

        if pieces:

            @pl.when(at == 0)
            def _():
                copies = []
                k = 0
                for parts, stack in zip(weights, held, strict=True):
                    column = 0
                    for group, start, end in parts:
                        row = 0
                        for p in group:
                            copies.append(
                                pltpu.make_async_copy(
                                    sources[k].at[:, start:end],
                                    stack.at[
                                        pl.ds(row, p.shape[0]), pl.ds(column, end - start)
                                    ],
                                    sems[0].at[k],
                                )
                            )
                            row += p.shape[0]
                            k += 1
                        column += end - start
                for c in copies:
                    c.start()
                for c in copies:
                    c.wait()

        body(at, turn(at), ins, held, results, extra)

    out = pl.pallas_call(
        kernel,
        grid=(count,),
        in_specs=in_specs,
        out_specs=[spec(shape) if cut else whole(shape) for shape, _, cut in outs],
        out_shape=[jax.ShapeDtypeStruct(shape, kind) for shape, kind, _ in outs],
        scratch_shapes=[
            *[pltpu.VMEM(shape, bf16) for shape in stacks],
            *scratch,
            *([pltpu.SemaphoreType.DMA((len(pieces),))] if pieces else []),
        ],
        compiler_params=pltpu.CompilerParams(
            dimension_semantics=("arbitrary",), vmem_limit_bytes=vmem * MEBI
        ),
        cost_estimate=pl.CostEstimate(
            flops=int(flops * COST), bytes_accessed=0, transcendentals=0
        ),
    )(*arrays, *pieces)
    return out


def enter(ring, inputs, out_grad):
    rows, width = inputs.shape
    wide = width // ring.size
    if wide % 128:
        here = ring.pick(inputs, ring.into)
        normed, scale = normalize(here.astype(f32))
        return normed.astype(bf16), here, ring.pick(out_grad, ring.into), scale

    def kernel(into, in_ref, grad_ref, normed_ref, here_ref, grad_here_ref, scale_ref):
        values = in_ref[...].astype(f32)
        scale = lax.rsqrt(jnp.mean(values * values, axis=-1, keepdims=True) + NORM_EPS)
        scale_ref[...] = scale
        for i in range(ring.size):
            at = pl.ds(pl.multiple_of(into[i] * wide, 128), wide)
            to = slice(i * wide, (i + 1) * wide)
            part = in_ref[:, at]
            here_ref[:, to] = part
            normed_ref[:, to] = (part.astype(f32) * scale).astype(bf16)
            grad_here_ref[:, to] = grad_ref[:, at]

    return pl.pallas_call(
        kernel,
        in_specs=[pl.BlockSpec(memory_space=pltpu.SMEM)] + [pl.BlockSpec(inputs.shape)] * 2,
        out_shape=[jax.ShapeDtypeStruct(inputs.shape, bf16)] * 3
        + [jax.ShapeDtypeStruct((rows, 1), f32)],
        compiler_params=pltpu.CompilerParams(vmem_limit_bytes=60 * MEBI),
    )(jnp.stack(ring.into), inputs, out_grad)


def leave(ring, kind, function, *values):
    rows, width = values[0].shape
    wide = width // ring.size
    if wide % 128:
        return ring.pick(function(*values).astype(kind), ring.back)

    def kernel(into, *refs):
        result = function(*[r[...] for r in refs[:-1]]).astype(kind)
        for i in range(ring.size):
            at = pl.ds(pl.multiple_of(into[i] * wide, 128), wide)
            refs[-1][:, at] = result[:, i * wide : (i + 1) * wide]

    return pl.pallas_call(
        kernel,
        in_specs=[pl.BlockSpec(memory_space=pltpu.SMEM)] + [pl.BlockSpec(v.shape) for v in values],
        out_shape=jax.ShapeDtypeStruct((rows, width), kind),
        compiler_params=pltpu.CompilerParams(vmem_limit_bytes=60 * MEBI),
    )(jnp.stack(ring.into), *values)


def head(ref, h):
    return ref[:, h * HD : (h + 1) * HD]


def decay_of(column, row):
    causal = lax.broadcasted_iota(jnp.int32, (BLK, BLK), 0) >= lax.broadcasted_iota(
        jnp.int32, (BLK, BLK), 1
    )
    return jnp.where(causal, jnp.exp(jnp.minimum(column - row, 0.0)), 0.0)


def silu_slope(values):
    sigmoid_v = jax.nn.sigmoid(values)
    return sigmoid_v * (1.0 + values * (1.0 - sigmoid_v))


def keys_kernel(heads, at, block, ins, held, outs, extra):
    rows, mask, tail, factors, ending = ins
    pre_out, keys_out, values_out, scaled_out, terms_out, message_out = outs
    (state,) = extra
    wide = heads * HD

    @pl.when(at == 0)
    def _():
        state[...] = jnp.zeros_like(state)
        message_out[wide:, :] = ending[...]

    pre = dot(rows[...], held[0][...])
    key_pre, value_pre = pre[:, :wide], pre[:, wide:]
    pre_out[...] = key_pre
    keep = mask[...]
    keys = (jax.nn.silu(key_pre).astype(bf16) * keep).astype(bf16)
    values = (value_pre.astype(bf16) * keep).astype(bf16)
    keys_out[...] = keys
    values_out[...] = values
    for h in range(heads):
        part = slice(h * HD, (h + 1) * HD)
        scaled = (keys[:, part].astype(f32) * tail[:, h : h + 1]).astype(bf16)
        scaled_out[:, part] = scaled
        term = t_dot(scaled, values[:, part])
        terms_out[part, :] = term
        renewed = factors[block, h] * state[part, :] + term
        state[part, :] = renewed
        message_out[part, :] = renewed.astype(bf16)


def queries_kernel(heads, at, block, ins, held, outs, extra):
    rows, keys, values, column, row = ins
    pre_out, gate_out, queries_out, scaled_out, probs_out, inner_out = outs
    wide = heads * HD
    both = dot(rows[...], held[0][...])
    query_pre = both[:, :wide]
    pre_out[...] = query_pre
    gate_out[...] = both[:, wide:]
    queries = jax.nn.silu(query_pre).astype(bf16)
    queries_out[...] = queries
    for h in range(heads):
        here = queries[:, h * HD : (h + 1) * HD]
        sums = column[:, h : h + 1]
        scaled_out[:, h * HD : (h + 1) * HD] = (here.astype(f32) * jnp.exp(sums)).astype(bf16)
        decays = decay_of(sums, row[0, h : h + 1, :])
        probs = (dot_t(here, head(keys, h)) * decays).astype(bf16)
        probs_out[:, h * BLK : (h + 1) * BLK] = probs
        inner_out[:, h * HD : (h + 1) * HD] = dot(probs, head(values, h))


def lanes(values):
    total = values[:, :HD]
    for i in range(1, values.shape[1] // HD):
        total = total + values[:, i * HD : (i + 1) * HD]
    return total


def states_kernel(heads, at, block, ins, held, outs, extra):
    inner, scaled, terms, message, reach, factors, keep = ins
    mixed_out, squares_out, used_out = outs
    (state,) = extra
    size = reach.shape[0]

    @pl.when(at == 0)
    def _():
        for h in range(heads):
            total = reach[0, h] * message[0, h * HD : (h + 1) * HD, :].astype(f32)
            for i in range(1, size):
                total = total + reach[i, h] * message[i, h * HD : (h + 1) * HD, :].astype(f32)
            state[h * HD : (h + 1) * HD, :] = total

    parts = []
    for h in range(heads):
        now = state[h * HD : (h + 1) * HD, :]
        used = (keep[block] * now).astype(bf16)
        used_out[h * HD : (h + 1) * HD, :] = used
        state[h * HD : (h + 1) * HD, :] = factors[block, h] * now + terms[h * HD : (h + 1) * HD, :]
        parts.append(head(inner, h) + dot(head(scaled, h), used))
    mixed = jnp.concatenate(parts, axis=1)
    mixed_out[...] = mixed
    squares_out[...] = lanes(mixed * mixed)


def branch_kernel(at, block, ins, held, outs, extra):
    mixed, gate, scale = ins
    joined_out, branch_out = outs
    joined = (mixed[...] * scale[...] * gate[...]).astype(bf16)
    joined_out[...] = joined
    branch_out[...] = dot_t(joined, held[0][...]).astype(bf16)


def gates_kernel(at, block, ins, held, outs, extra):
    (rows,) = ins
    left_out, right_out, product_out = outs
    hidden = left_out.shape[1]
    gates = dot(rows[...], held[0][...])
    left, right = gates[:, :hidden], gates[:, hidden:]
    left_out[...] = left
    right_out[...] = right
    product_out[...] = (left * right).astype(bf16)


def gates_back_kernel(at, block, ins, held, outs, extra):
    rows, left, right = ins
    (both_out,) = outs
    hidden = left.shape[1]
    product_grad = dot(rows[...], held[0][...])
    both_out[:, :hidden] = (product_grad * right[...]).astype(bf16)
    both_out[:, hidden:] = (product_grad * left[...]).astype(bf16)


def back_kernel(at, block, ins, held, outs, extra):
    total = dot_t(ins[0][...], held[0][...])
    for i, stack in zip(ins[1:], held[1:], strict=True):
        total = total + dot_t(i[...], stack[...])
    outs[0][...] = total.astype(bf16)


def joined_back_kernel(at, block, ins, held, outs, extra):
    rows, mixed, gate, scale = ins
    gate_out, inward_out, dots_out = outs
    joined_grad = dot(rows[...], held[0][...])
    normed = mixed[...] * scale[...]
    gate_out[...] = (joined_grad * normed).astype(bf16)
    inward = joined_grad * gate[...]
    inward_out[...] = inward
    dots_out[...] = lanes(inward * normed)


def mixed_back_kernel(heads, at, block, ins, held, outs, extra):
    inward, mixed, scale, dots, scaled, factors, keep = ins
    grad_out, kept_out, back_out = outs
    (state,) = extra
    normed = mixed[...] * scale[...]
    grad = (scale[...] * (inward[...] - normed * dots[...])).astype(bf16)
    grad_out[...] = grad

    @pl.when(at == 0)
    def _():
        state[...] = jnp.zeros_like(state)

    for h in range(heads):
        part = slice(h * HD, (h + 1) * HD)
        kept = keep[block] * t_dot(head(scaled, h), grad[:, part])
        kept_out[part, :] = kept
        renewed = factors[block, h] * state[part, :] + kept
        state[part, :] = renewed
        back_out[part, :] = renewed.astype(bf16)


def scores_back_kernel(heads, at, block, ins, held, outs, extra):
    grad, keys, values, queries, probs, used, query_pre, column, row = ins
    query_out, key_out, value_out = outs
    for h in range(heads):
        part = slice(h * HD, (h + 1) * HD)
        here = grad[:, part]
        sums = column[:, h : h + 1]
        score = (dot_t(here, values[:, part]) * decay_of(sums, row[0, h : h + 1, :])).astype(bf16)
        query_grad = dot(score, keys[:, part]) + dot_t(here, used[part, :]) * jnp.exp(sums)
        query_out[:, part] = (query_grad * silu_slope(query_pre[:, part])).astype(bf16)
        key_out[:, part] = t_dot(score, queries[:, part])
        value_out[:, part] = t_dot(probs[:, h * BLK : (h + 1) * BLK], here)


def states_back_kernel(heads, at, block, ins, held, outs, extra):
    key_grad, value_grad, query, gate, values, scaled, kept, message = ins[:8]
    key_pre, mask, tail, reach, factors = ins[8:]
    pair_out, other_out = outs
    (state,) = extra
    size = reach.shape[0]
    wide = heads * HD

    @pl.when(at == 0)
    def _():
        for h in range(heads):
            total = reach[0, h] * message[0, h * HD : (h + 1) * HD, :].astype(f32)
            for i in range(1, size):
                total = total + reach[i, h] * message[i, h * HD : (h + 1) * HD, :].astype(f32)
            state[h * HD : (h + 1) * HD, :] = total

    keep = mask[...]
    for h in range(heads):
        part = slice(h * HD, (h + 1) * HD)
        now = state[part, :]
        low = now.astype(bf16)
        key = key_grad[:, part] + dot_t(values[:, part], low) * tail[:, h : h + 1]
        pair_out[:, part] = (key * keep * silu_slope(key_pre[:, part])).astype(bf16)
        value = value_grad[:, part] + dot(scaled[:, part], low)
        pair_out[:, wide + h * HD : wide + (h + 1) * HD] = (value * keep).astype(bf16)
        state[part, :] = factors[block, h] * now + kept[part, :]
    other_out[:, :wide] = query[...]
    other_out[:, wide:] = gate[...]


COST = 0.0


def mm(spec, a, b):
    return jnp.einsum(spec, a, b, preferred_element_type=f32)


def scatter_rows(value):
    return lax.psum_scatter(value, "tp", scatter_dimension=0, tiled=True)


def gather_rows(value):
    return lax.all_gather(value, "tp", axis=0, tiled=True)


def adamw_step(weight, first, second, gradient):
    first_new = BETA_ONE * first + (1.0 - BETA_ONE) * gradient
    second_new = BETA_TWO * second + (1.0 - BETA_TWO) * gradient * gradient
    fix_one = 1.0 - BETA_ONE**STEP
    fix_two = 1.0 - BETA_TWO**STEP
    update = first_new / fix_one / (jnp.sqrt(second_new / fix_two) + ADAM_EPS)
    return (weight - LEARN_RATE * (update + WEIGHT_DECAY * weight), first_new, second_new)


def adamw_across(weight, first, second, gradient):
    rows, columns = weight.shape
    part = 128

    def kernel(w, m, v, g, w_out, m_out, v_out):
        results = adamw_step(w[...], m[...], v[...], g[...].T)
        for ref, value in zip((w_out, m_out, v_out), results, strict=True):
            ref[...] = value

    here = pl.BlockSpec((part, columns), lambda i: (i, 0))
    return pl.pallas_call(
        kernel,
        grid=(rows // part,),
        in_specs=[here] * 3 + [pl.BlockSpec((columns, part), lambda i: (0, i))],
        out_specs=[here] * 3,
        out_shape=[jax.ShapeDtypeStruct(weight.shape, f32)] * 3,
        compiler_params=pltpu.CompilerParams(vmem_limit_bytes=60 * MEBI),
    )(weight, first, second, gradient)


def solution(mesh):
    size = mesh.shape["seq"]

    def local(
        inputs,
        out_grad,
        seq_lengths,
        log_decay,
        mixer_weight,
        output_weight,
        glu_weight,
        down_weight,
        mixer_first,
        output_first,
        glu_first,
        down_first,
        mixer_second,
        output_second,
        glu_second,
        down_second,
    ):
        rows = log_decay.shape[0]
        heads = log_decay.shape[1]
        blocks = rows // BLK
        wide = heads * HD
        hidden = down_weight.shape[0]
        ring = Ring(size)
        ring.place()
        half = ring.half
        seq_place = lax.axis_index("seq")
        keep_flags, token_mask = layout(seq_lengths, seq_place * blocks, blocks)
        mask_col = token_mask[:, None].astype(f32)

        output_low = output_weight.astype(bf16).T
        down_low = down_weight.astype(bf16).T
        pair, part = 2 * wide, wide // 2
        cut = hidden // 256 * 128
        mixer_lanes = [
            jnp.concatenate(
                [mixer_weight[i].astype(bf16), mixer_weight[j].astype(bf16), output_low[:, a:b]], axis=1
            )
            for i, j, a, b in ((1, 2, 0, part), (0, 3, part, wide))
        ]
        mixer = [Line(ring, spread(ring, low, i)) for i, low in enumerate(mixer_lanes)]
        glu = [Line(ring, spread(ring, glu_weight[i].astype(bf16), i)) for i in range(2)]
        down = [
            Line(ring, spread(ring, low, i))
            for i, low in enumerate((down_low[:, :cut], down_low[:, cut:]))
        ]

        rows_one_here, inputs_here, out_grad_here, scale_one = enter(ring, inputs, out_grad)
        rows_one = gather_rows(rows_one_here)
        grad_rows = gather_rows(out_grad_here)

        lower = (jnp.arange(BLK)[:, None] >= jnp.arange(BLK)[None, :]).astype(f32)
        cumulative = jnp.einsum(
            "ts,bsh->bth",
            lower,
            log_decay.reshape(blocks, BLK, heads),
            precision=lax.Precision.HIGHEST,
        )
        block_ends = cumulative[:, -1, :]
        tail = jnp.exp(block_ends[:, None, :] - cumulative).reshape(rows, heads)
        column = cumulative.reshape(rows, heads)
        row = jnp.transpose(cumulative, (0, 2, 1))
        factors = keep_flags[:, None] * jnp.exp(block_ends)

        turns(mixer, half)
        mixer_full = [lane.end() for lane in mixer]
        pair_stack, other_stack = [[(full, 0, pair)] for full in mixer_full]
        output_stack = [(full, pair, pair + part) for full in mixer_full]
        turns(glu, 1, *[lane.got[-1][0] for lane in mixer])

        state_shape = (blocks * wide, HD)
        factor = factors[0]
        for j in range(1, blocks):
            factor = factor * factors[j]
        first = factor.astype(bf16)
        second = (factor - first.astype(f32)).astype(bf16)
        third = (factor - first.astype(f32) - second.astype(f32)).astype(bf16)
        ending = jnp.pad(jnp.stack([first, second, third]), ((0, 13), (0, HD - heads)))
        key_pre, keys, values, scaled_k, terms, message = by_block(
            functools.partial(keys_kernel, heads),
            [
                Rows(then(mixer, half, rows_one)),
                Rows(mask_col),
                Rows(tail),
                Scalars(factors),
                ending,
            ],
            [pair_stack],
            [
                ((rows, wide), f32, True),
                ((rows, wide), bf16, True),
                ((rows, wide), bf16, True),
                ((rows, wide), bf16, True),
                (state_shape, f32, True),
                ((wide + 16, HD), bf16, False),
            ],
            [pltpu.VMEM((wide, HD), f32)],
            flops=2 * rows * D * 2 * wide,
        )
        message, grad_rows = then(glu[:1], 1, message, grad_rows)
        message = lax.all_gather(message, "seq")
        all_factors = jnp.sum(message[:, wide : wide + 3, :heads].astype(f32), axis=1)
        place = jnp.arange(size)

        def reach(between):
            picked = jnp.where(between[:, :, None], all_factors[None, :, :], 1.0)
            total = picked[:, 0]
            for i in range(1, size):
                total = total * picked[:, i]
            return total

        from_before = jnp.where(
            (place < seq_place)[:, None],
            reach((place[None, :] > place[:, None]) & (place[None, :] < seq_place)),
            0.0,
        )
        from_after = jnp.where(
            (place > seq_place)[:, None],
            reach((place[None, :] < place[:, None]) & (place[None, :] > seq_place)),
            0.0,
        )
        query_pre, gate_u, queries, scaled_q, probs, inner = by_block(
            functools.partial(queries_kernel, heads),
            [Rows(rows_one), Rows(keys), Rows(values), Rows(column), Rows(row)],
            [other_stack],
            [
                ((rows, wide), f32, True),
                ((rows, wide), f32, True),
                ((rows, wide), bf16, True),
                ((rows, wide), bf16, True),
                ((rows, heads * BLK), bf16, True),
                ((rows, wide), f32, True),
            ],
            flops=2 * rows * D * 2 * wide,
        )
        turns(glu, 1, inner)
        mixer_out, squares, used = by_block(
            functools.partial(states_kernel, heads),
            [
                Rows(inner),
                Rows(scaled_q),
                Rows(terms),
                message,
                Scalars(from_before),
                Scalars(factors),
                Scalars(keep_flags),
            ],
            [],
            [((rows, wide), f32, True), ((rows, HD), f32, True), (state_shape, bf16, True)],
            [pltpu.VMEM((wide, HD), f32)],
            flops=2 * rows * D * wide // 4,
        )
        turns(glu[:1], half - 3)
        turns(glu[1:], half - 3, squares)
        squares = lax.psum(jnp.sum(squares, axis=1), "tp")
        mixer_scale = lax.rsqrt(squares / D + NORM_EPS)[:, None]
        joined, branch_here = by_block(
            branch_kernel,
            [Rows(mixer_out), Rows(gate_u), Rows(mixer_scale)],
            [output_stack],
            [((rows, wide), bf16, True), ((rows, D), bf16, True)],
            flops=2 * rows * D * wide,
        )
        turns(glu, 1, branch_here)
        turns(down, 1)
        branch = scatter_rows(then(glu[:1], 3, branch_here))
        middle = inputs_here.astype(f32) + then(glu, half - 1, branch).astype(f32)
        normed_two, scale_two = normalize(middle)
        rows_two_here = normed_two.astype(bf16)
        rows_two = gather_rows(rows_two_here)
        turns(down, half - 3, rows_two_here)
        rows_two = then(down, 1, rows_two)

        glu_stack = [(lane.end(), 0, hidden) for lane in glu]
        gate_left, gate_right, product = by_block(
            gates_kernel,
            [Rows(rows_two)],
            [glu_stack],
            [((rows, hidden), f32, True), ((rows, hidden), f32, True), ((rows, hidden), bf16, True)],
            flops=2 * rows * D * 2 * hidden,
        )

        turns(down, 1, product)
        turns(down, 1)
        down_parts = [lane.end() for lane in down]
        down_stack = [(full, 0, full[0].shape[1]) for full in down_parts]
        down_total = [
            Line(
                ring,
                collect(
                    ring,
                    lambda off, cols=cols: [mm("td,tc->dc", ring.columns(grad_rows, off), cols)],
                    i,
                ),
            )
            for i, cols in enumerate((product[:, :cut], product[:, cut:]))
        ]
        turns(down_total, 1)
        (both_grads,) = by_block(
            gates_back_kernel,
            [Rows(grad_rows), Rows(gate_left), Rows(gate_right)],
            [down_stack],
            [((rows, 2 * hidden), bf16, True)],
            flops=2 * rows * D * hidden,
        )
        both_grads = then(down_total, 0, both_grads)
        turns(down_total, 1)
        glu_total = [
            Line(
                ring,
                collect(
                    ring,
                    lambda off, cols=cols: [mm("td,tc->dc", ring.columns(rows_two, off), cols)],
                    i,
                ),
            )
            for i, cols in enumerate((both_grads[:, :hidden], both_grads[:, hidden:]))
        ]
        turns(glu_total, 1)
        (two_here,) = by_block(
            back_kernel,
            [Rows(behind(glu_total, 1, both_grads))],
            [glu_stack],
            [((rows, D), bf16, True)],
            flops=2 * rows * D * 2 * hidden,
        )
        two_grad = scatter_rows(then(down_total, 2, two_here))
        turns(down_total, half - 2)
        two_grad = behind(down_total, half, then(down_total, half - 1, two_grad))
        middle_grad = out_grad_here.astype(f32) + norm_back(
            normed_two, scale_two, two_grad.astype(f32)
        )
        branch_grad = gather_rows(middle_grad.astype(bf16))
        turns(glu_total, 1)
        branch_grad = then(glu_total[:1], 0, branch_grad)

        gate_grad, inward, dots = by_block(
            joined_back_kernel,
            [Rows(branch_grad), Rows(mixer_out), Rows(gate_u), Rows(mixer_scale)],
            [output_stack],
            [((rows, wide), bf16, True), ((rows, wide), f32, True), ((rows, HD), f32, True)],
            flops=2 * rows * D * wide,
        )
        turns(glu_total, half - 2)
        dots = then(glu_total[1:], 2, dots)
        row_dots = (lax.psum(jnp.sum(dots, axis=1), "tp") / D)[:, None]
        mixed_grad, kept, back = by_block(
            functools.partial(mixed_back_kernel, heads),
            [
                Rows(inward),
                Rows(mixer_out),
                Rows(mixer_scale),
                Rows(row_dots),
                Rows(scaled_q),
                Scalars(factors),
                Scalars(keep_flags),
            ],
            [],
            [((rows, wide), bf16, True), (state_shape, f32, True), ((wide, HD), bf16, False)],
            [pltpu.VMEM((wide, HD), f32)],
            backward=True,
            flops=2 * rows * D * wide // 4,
        )
        all_back = lax.all_gather(back, "seq")
        (feed_here,) = by_block(
            back_kernel,
            [Rows(lax.optimization_barrier((product, back))[0])],
            [down_stack],
            [((rows, D), bf16, True)],
            flops=2 * rows * D * hidden,
        )
        feed_here = then(glu_total[:1], 3, feed_here)
        query_back, key_grad, value_grad = by_block(
            functools.partial(scores_back_kernel, heads),
            [
                Rows(lax.optimization_barrier((mixed_grad, feed_here))[0]),
                Rows(keys),
                Rows(values),
                Rows(queries),
                Rows(probs),
                Rows(used),
                Rows(query_pre),
                Rows(column),
                Rows(row),
            ],
            [],
            [((rows, wide), bf16, True), ((rows, wide), f32, True), ((rows, wide), f32, True)],
            flops=2 * rows * D * wide,
        )
        query_back = then(glu_total[1:], 3, query_back)
        feed_out = scatter_rows(lax.optimization_barrier((feed_here, all_back))[0])
        pair_grads, other_grads = by_block(
            functools.partial(states_back_kernel, heads),
            [
                Rows(key_grad),
                Rows(value_grad),
                Rows(query_back),
                Rows(gate_grad),
                Rows(values),
                Rows(scaled_k),
                Rows(kept),
                then(glu_total[1:], 1, all_back),
                Rows(key_pre),
                Rows(mask_col),
                Rows(tail),
                Scalars(from_after),
                Scalars(factors),
            ],
            [],
            [((rows, pair), bf16, True), ((rows, pair), bf16, True)],
            [pltpu.VMEM((wide, HD), f32)],
            backward=True,
            flops=2 * rows * D * wide // 4,
        )
        pair_grads, other_grads = then(glu_total, half, pair_grads, other_grads)
        mixer_total = [
            Line(
                ring,
                collect(
                    ring,
                    lambda off, grads=grads, cols=cols: [
                        mm("td,tc->dc", ring.columns(rows_one, off), grads),
                        mm("td,tc->dc", ring.columns(branch_grad, off), cols),
                    ],
                    i,
                ),
            )
            for i, (grads, cols) in enumerate(
                ((pair_grads, joined[:, :part]), (other_grads, joined[:, part:]))
            )
        ]
        turns(mixer_total, half - 1)
        block_out = leave(ring, bf16, lambda a, b: a + b.astype(f32), middle, feed_out)
        (one_here,) = by_block(
            back_kernel,
            [Rows(behind(mixer_total, 1, pair_grads)), Rows(other_grads)],
            [pair_stack, other_stack],
            [((rows, D), bf16, True)],
            flops=2 * rows * D * 4 * wide,
        )
        one_grad = scatter_rows(then(mixer_total, 1, one_here))
        one_grad = then(mixer_total, half - 1, one_grad)
        input_grad = leave(
            ring,
            f32,
            lambda grad, rows, scale, incoming: (
                grad + norm_back(rows.astype(f32) * scale, scale, incoming.astype(f32))
            ),
            middle_grad,
            inputs_here,
            scale_one,
            one_grad,
        )

        turns(mixer_total, 1)
        down_sum = jnp.concatenate([lane.end()[0] for lane in down_total], axis=1)
        glu_sum = jnp.stack([lane.end()[0] for lane in glu_total])
        (pair_sum, first_sum), (other_sum, second_sum) = [lane.end() for lane in mixer_total]
        output_sum = jnp.concatenate([first_sum, second_sum], axis=1)

        mixer_sum = jnp.stack(
            [other_sum[:, :wide], pair_sum[:, :wide], pair_sum[:, wide:], other_sum[:, wide:]]
        )
        mixer_new, mixer_first_new, mixer_second_new = adamw_step(
            mixer_weight, mixer_first, mixer_second, mixer_sum
        )
        output_new, output_first_new, output_second_new = adamw_across(
            output_weight, output_first, output_second, output_sum
        )
        glu_new, glu_first_new, glu_second_new = adamw_step(
            glu_weight, glu_first, glu_second, then(mixer_total, 1, glu_sum)
        )
        down_new, down_first_new, down_second_new = adamw_across(
            down_weight, down_first, down_second, then(mixer_total, 1, down_sum)
        )
        return (
            block_out,
            input_grad,
            mixer_new,
            output_new,
            glu_new,
            down_new,
            mixer_first_new,
            output_first_new,
            glu_first_new,
            down_first_new,
            mixer_second_new,
            output_second_new,
            glu_second_new,
            down_second_new,
        )

    rows = P(("seq", "tp"), None)
    deep, tall = P(None, "seq", "tp"), P("tp", "seq")
    weights = (deep, tall, deep, tall)
    in_specs = (rows, rows, P(), P("seq", "tp"), *weights * 3)
    out_specs = (rows, rows, *weights * 3)
    return jax.shard_map(local, mesh=mesh, in_specs=in_specs, out_specs=out_specs, check_vma=False)
```
